256 devices in a mesh: seq: 64 (over x, z, core), tp: 4 (over y).
Axes of the slice: x: 4, y: 4, z: 8, core: 2. Of those that a mesh axis runs over, the one named last changes fastest.
Arguments:
- inputs: bfloat16 [32768, 6144], P('seq'), may hold values from -6 to 6
- proj_weight: bfloat16 [4, 6144, 1024], P(None, 'seq', 'tp'), may hold values from -0.078125 to 0.078125
- decay_codes: int32 [8], P('tp'), may hold values from 1 to 32768, as said below
- norm_gain: float32 [1024], P('tp'), may hold values from 0.1 to 1.9
- out_weight: bfloat16 [1024, 6144], P('seq', 'tp'), may hold values from -0.1875 to 0.1875
Outputs:
- mixed: bfloat16 [32768, 6144], P('seq', 'tp')
The draws below stay inside these ranges and needn't reach their ends.
Inputs may be any that keep to these rules, and one draw needn't show every extreme that they name: `decay_codes`: each is a power of 8.
All inputs are finite; a program needn't handle non-finite values.
Results may differ from the reference program's by a relative error of at most 0.0052.
Values may be sent and summed in bfloat16 or wider, within the bound.
A program may use at most 64 MiB of HBM per device.

```python
import jax
import jax.numpy as jnp
from jax import lax

D = 6144
HEAD_DIM = 128
HEADS = 8
TOK_DEV = 512
HH = 1024
TOKENS = 32768
N_SEQ = 64


def draw_decay_codes(key, part):
    key = jax.random.fold_in(key, 7)
    power_key = jax.random.fold_in(key, 1)
    order_key = jax.random.fold_in(key, 2)
    power = jax.random.randint(power_key, (HEADS,), 0, 6)
    order = jax.random.permutation(order_key, HEADS)
    power = power.at[order[0]].set(5)
    power = power.at[order[1]].set(0)
    return jnp.power(8, power).astype(jnp.int32)


def shard_levels(stream_key, shape, shards, smallest, high):
    level = 1.0
    for position, shards_of in shards:
        heights = jax.random.uniform(jax.random.fold_in(jax.random.fold_in(stream_key, 6), position), (shards_of,), jnp.float32, smallest / len(shards), high / len(shards))
        level = level * jnp.repeat(jnp.exp(heights), shape[position] // shards_of).reshape((-1,) + (1,) * (len(shape) - 1 - position))
    return level


def gaussian(rng, extent, spread, limit, cuts=(), dtype=jnp.bfloat16):
    factor_of = shard_levels(rng, extent, cuts, -0.22, 0.18) if cuts else 1.0
    drawn = jax.random.normal(rng, extent, jnp.float32) * spread * factor_of
    return jnp.minimum(jnp.maximum(drawn, -limit), limit).astype(dtype)


def setup_inputs(seed: int = 0) -> dict:
    key_list = jax.random.split(jax.random.key(seed), 6)
    inputs = gaussian(key_list[0], (TOKENS, D), 1.0, 6.0, ((0, 64),))
    proj_weight = gaussian(key_list[1], (4, D, HH), D ** -0.5, 0.078125, ((1, 64), (2, 4)))
    decay_codes = draw_decay_codes(jax.random.fold_in(key_list[5], 71), 0)
    norm_gain = jnp.clip(1.0 + 0.18 * jax.random.normal(key_list[3], (HH,), jnp.float32), 0.1, 1.9)
    out_weight = gaussian(key_list[4], (HH, D), HH ** -0.5, 0.1875, ((0, 64), (1, 4)))
    return {"inputs": inputs, "proj_weight": proj_weight, "decay_codes": decay_codes, "norm_gain": norm_gain, "out_weight": out_weight}


def reference(inputs, proj_weight, decay_codes, norm_gain, out_weight):
    high = lax.Precision.HIGHEST
    log_decay = jnp.log1p(-decay_codes.astype(jnp.float32) * 1e-06)
    length = TOK_DEV
    pos = jnp.arange(length).astype(jnp.float32)
    diff = pos[:, None] - pos[None, :]
    causal = diff >= 0
    weights = jnp.where(causal[None], jnp.exp(jnp.maximum(diff, 0.0)[None] * log_decay[:, None, None]), 0.0)
    into = jnp.exp((pos + 1.0)[None, :] * log_decay[:, None])
    tail = jnp.exp((length - 1.0 - pos)[None, :] * log_decay[:, None])
    whole = jnp.exp(length * log_decay)
    blocks = inputs.reshape(N_SEQ, length, D)

    def step(state, rows):
        proj = jnp.stack([jnp.dot(rows, proj_weight[a], preferred_element_type=jnp.float32) for a in range(4)])
        acts = jax.nn.silu(proj[:3]).astype(jnp.bfloat16)
        heads = acts.reshape(3, length, HEADS, HEAD_DIM).transpose(0, 2, 1, 3).astype(jnp.float32)
        query, keys, values = (heads[0], heads[1], heads[2])
        scores = jnp.einsum('htd,hsd->hts', query, keys) * weights
        probs = scores.astype(jnp.bfloat16).astype(jnp.float32)
        intra = jnp.einsum('hts,hsd->htd', probs, values)
        inter = jnp.einsum('htd,hde->hte', query * into[:, :, None], state, precision=high)
        attended = intra + inter
        scale = lax.rsqrt(lax.optimization_barrier(jnp.mean(attended * attended, axis=2, keepdims=True)) + 1e-06)
        normed = (attended * scale).transpose(1, 0, 2).reshape(length, HH)
        hidden = (normed * norm_gain[None, :] * jax.nn.sigmoid(proj[3])).astype(jnp.bfloat16)
        local_state = jnp.einsum('hsd,hse->hde', keys * tail[:, :, None], values, precision=high)
        new_state = whole[:, None, None] * state + local_state
        out = jnp.dot(hidden, out_weight, preferred_element_type=jnp.float32).astype(jnp.bfloat16)
        return (new_state, out)
    start = jnp.zeros((HEADS, HEAD_DIM, HEAD_DIM), jnp.float32)
    _, outs = lax.scan(step, start, blocks)
    return outs.reshape(TOKENS, D)
```

```python
import functools

import jax
import jax.numpy as jnp
from jax import lax
from jax.experimental import pallas as pl
from jax.experimental.pallas import tpu as pltpu
from jax.sharding import PartitionSpec as P

NX, NZ, NY = 4, 8, 4
T = 512
D = 6144
HD = 128
F = 256
SH = 96
KX = D // NX
MESH = pl.DeviceIdType.MESH
BF = jnp.bfloat16
F32 = jnp.float32

GROUPS = ((0, 2, 32), (2, 1, 32), (3, 1, 48), (4, 1, 48))
OFFSETS = (0, 3, 6, 9)
STAGES = 7
NSLOT = 40


def kernel(x_hbm, wp_hbm, codes, gain_ref, wo_hbm, out_hbm,
           buf, xv, wts, acc, kv, qv, att, hid, oacc, outv,
           state, sx, snd, rcv, stg, pri,
           load_sem, own_send, own_recv, recv, relay_recv, send_sem,
           st_send, st_recv, h_send, h_recv, out_sem):
    s = lax.axis_index("seq")
    y = lax.axis_index("tp")
    x, z, c = s // 16, (s // 2) % 8, s % 2
    q = s // 2

    def dev(px, pz, pc, py):
        return {"seq": (px * NZ + pz) * 2 + pc, "tp": py}

    xp, xm = (x + 1) % NX, (x + 3) % NX
    zp, zm = (z + 1) % NZ, (z + 7) % NZ
    yp, ym = (y + 1) % NY, (y + 3) % NY
    x2, z4, y2 = (x + 2) % NX, (z + 4) % NZ, (y + 2) % NY
    sib = dev(x, z, 1 - c, y)
    to = {"xp": dev(xp, z, c, y), "xm": dev(xm, z, c, y), "zp": dev(x, zp, c, y), "zm": dev(x, zm, c, y)}
    to_yp, to_ym = dev(x, z, c, yp), dev(x, z, c, ym)
    z_1 = z + 1 - 2 * (z % 2)
    z_2 = z + 2 - 4 * ((z // 2) % 2)
    x_1 = x + 1 - 2 * (x % 2)
    partners = (dev(x, z_1, c, y), dev(x, z_2, c, y), dev(x, z4, c, y), dev(x_1, z, c, y), dev(x2, z, c, y))

    x_load = pltpu.make_async_copy(x_hbm, xv, load_sem.at[0])
    x_load.start()
    loads = [
        [pltpu.make_async_copy(wp_hbm.at[pl.ds(1, 2)], buf.at[pl.ds(0, 2), x, z, c], load_sem.at[1])],
        [pltpu.make_async_copy(wp_hbm.at[pl.ds(0, 1)], buf.at[pl.ds(2, 1), x, z, c], load_sem.at[2])],
        [pltpu.make_async_copy(wp_hbm.at[pl.ds(3, 1)], buf.at[pl.ds(3, 1), x, z, c], load_sem.at[3])],
        [pltpu.make_async_copy(wo_hbm.at[:, pl.ds(F * j, F)], buf.at[4, x, z, c, pl.ds(16 * j, 16), :], load_sem.at[4 + j])
         for j in range(6)],
    ]
    for group in loads:
        for copy in group:
            copy.start()

    barrier = pltpu.get_barrier_semaphore()
    greet = list(to.values()) + [sib, to_yp, to_ym, partners[1], partners[2], partners[4]]
    for other in greet:
        pl.semaphore_signal(barrier, inc=1, device_id=other, device_id_type=MESH)
    pl.semaphore_wait(barrier, len(greet))

    def rcopy(src, dst, ssem, rsem, device):
        return pltpu.make_async_remote_copy(src, dst, ssem, rsem, device_id=device, device_id_type=MESH)

    def own_copy(g):
        i0, n, _ = GROUPS[g]
        ref = buf.at[pl.ds(i0, n), x, z, c]
        return rcopy(ref, ref, own_send.at[g], own_recv.at[g], sib)

    for g in range(len(GROUPS)):
        for copy in loads[g]:
            copy.wait()
        own_copy(g).start()

    pos = lambda shape, dim: lax.broadcasted_iota(jnp.int32, shape, dim).astype(F32)
    log_decay = [jnp.log1p(-(jnp.full((1, HD), codes[h], jnp.int32).astype(F32)) * 1e-06) for h in range(2)]
    ld_mine = jnp.where(c == 0, log_decay[0], log_decay[1])

    def table(r, carry):
        row = pos((64, T), 0) + (r * 64).astype(F32)
        diff = row - pos((64, T), 1)
        for h in range(2):
            ld = jnp.concatenate([log_decay[h]] * (T // HD), axis=1)
            w = jnp.where(diff >= 0, jnp.exp(jnp.maximum(diff, 0.0) * ld), 0.0)
            wts[h, pl.ds(pl.multiple_of(r * 64, 64), 64), :] = w
        return carry

    def piece(g, px, pz, rows, half=None):
        i0, n, _ = GROUPS[g]
        cc = pl.ds(0, 2) if half is None else pl.ds(half, 1)
        return buf.at[pl.ds(i0, n), px, pz, cc, pl.ds(*rows), :]

    def send(g, kind, ref, slot, where):
        rcopy(ref, ref, send_sem.at[g, kind], recv.at[g, slot], to[where]).start()

    def arrived(g, ref, slot):
        rcopy(ref, ref, send_sem.at[g, 0], recv.at[g, slot], sib).wait_recv()

    def relay(g, kind, ref):
        rcopy(ref, ref, send_sem.at[g, 2 + kind], relay_recv.at[g, kind], sib).start()

    def stage_a(g, t):
        i0, n, a = GROUPS[g]
        rows = (0, a)
        pc = functools.partial(piece, g, rows=rows)
        if t == 0:
            send(g, 0, pc(x, z), 0, "xp")
            send(g, 0, pc(x, z), 1, "xm")
        if t == 1:
            arrived(g, pc(xm, z), 0)
            send(g, 0, pc(xm, z, half=0), 2, "xp")
            arrived(g, pc(xp, z), 1)
            send(g, 0, pc(xp, z, half=1), 3, "xm")
        if t == 2:
            arrived(g, pc(x2, z, half=0), 2)
            arrived(g, pc(x2, z, half=1), 3)
        for k, (px, start) in reversed(list(enumerate(((x, 0), (xm, 1), (xp, 1), (x2, 2))))):
            h = t - start
            slot = lambda hop, way: 4 + (k * 4 + hop) * 2 + way
            down, up = (z + 8 - h) % NZ, (z + h) % NZ
            if h == 0:
                send(g, 1, pc(px, z), slot(0, 0), "zp")
                send(g, 1, pc(px, z), slot(0, 1), "zm")
            elif 1 <= h <= 3:
                arrived(g, pc(px, down), slot(h - 1, 0))
                send(g, 1, pc(px, down, half=None if h < 3 else 0), slot(h, 0), "zp")
                arrived(g, pc(px, up), slot(h - 1, 1))
                send(g, 1, pc(px, up, half=None if h < 3 else 1), slot(h, 1), "zm")
            elif h == 4:
                arrived(g, pc(px, z4, half=0), slot(3, 0))
                arrived(g, pc(px, z4, half=1), slot(3, 1))
        if t == 1:
            relay(g, 0, pc(xm, z))
            relay(g, 0, pc(xp, z))
        if t == 2:
            relay(g, 0, pc(x2, z))
        if t >= 3:
            h = t - 2
            line = lambda pz: buf.at[pl.ds(i0, n), :, pz, :, pl.ds(*rows), :]
            relay(g, 1, line((z + 8 - h) % NZ))
            if h < 4:
                relay(g, 1, line((z + h) % NZ))

    def stage_b(g, t):
        i0, n, a = GROUPS[g]
        rows = (a, SH - a)
        pc = functools.partial(piece, g, rows=rows)
        down, up = (z + 8 - t) % NZ, (z + t) % NZ
        if t == 0:
            send(g, 0, pc(x, z), 0, "zp")
            send(g, 0, pc(x, z), 1, "zm")
        elif t <= 3:
            arrived(g, pc(x, down), 2 * t - 2)
            send(g, 0, pc(x, down, half=None if t < 3 else 0), 2 * t, "zp")
            arrived(g, pc(x, up), 2 * t - 1)
            send(g, 0, pc(x, up, half=None if t < 3 else 1), 2 * t + 1, "zm")
        elif t == 4:
            arrived(g, pc(x, z4, half=0), 6)
            arrived(g, pc(x, z4, half=1), 7)
        chains = ((0, 0), (7, 1), (1, 1), (6, 2), (2, 2), (5, 3), (3, 3), (4, 4))
        for k, (dz, start) in reversed(list(enumerate(chains))):
            j = t - start
            pz = (z + dz) % NZ
            slot = 8 + 4 * k
            if j == 0:
                send(g, 1, pc(x, pz), slot, "xp")
                send(g, 1, pc(x, pz), slot + 1, "xm")
            elif j == 1:
                arrived(g, pc(xm, pz), slot)
                send(g, 1, pc(xm, pz, half=0), slot + 2, "xp")
                arrived(g, pc(xp, pz), slot + 1)
                send(g, 1, pc(xp, pz, half=1), slot + 3, "xm")
            elif j == 2:
                arrived(g, pc(x2, pz, half=0), slot + 2)
                arrived(g, pc(x2, pz, half=1), slot + 3)
        if 1 <= t <= 3:
            relay(g, 0, pc(x, down))
            relay(g, 0, pc(x, up))
        if t == 4:
            relay(g, 0, pc(x, z4))
        line = lambda px: buf.at[pl.ds(i0, n), px, :, :, pl.ds(*rows), :]
        if t == 5:
            relay(g, 1, line(xm))
            relay(g, 1, line(xp))
        if t == 6:
            relay(g, 1, line(x2))

    def stage(g, t):
        if t == 0:
            i0, n, _ = GROUPS[g]
            ref = buf.at[pl.ds(i0, n), x, z, 1 - c]
            rcopy(ref, ref, own_send.at[g], own_recv.at[g], sib).wait_recv()

        @pl.when(c == 0)
        def _():
            stage_a(g, t)

        @pl.when(c == 1)
        def _():
            stage_b(g, t)

    def sizes(g, core):
        i0, n, a = GROUPS[g]
        if core == 0:
            return [buf.at[pl.ds(i0, n), pl.ds(0, 3), 0, :, pl.ds(0, a), :],
                    buf.at[pl.ds(i0, n), :, pl.ds(0, 7), :, pl.ds(0, a), :]]
        return [buf.at[pl.ds(i0, n), 0, pl.ds(0, 7), :, pl.ds(a, SH - a), :],
                buf.at[pl.ds(i0, n), pl.ds(0, 3), :, :, pl.ds(a, SH - a), :]]

    def relays_arrived(g):
        for core in range(2):
            @pl.when(c == 1 - core)
            def _(core=core):
                for kind, ref in enumerate(sizes(g, core)):
                    rcopy(ref, ref, send_sem.at[g, 0], relay_recv.at[g, kind], sib).wait_recv()

    def sends_done(g):
        own_copy(g).wait_send()
        for core in range(2):
            @pl.when(c == core)
            def _(core=core):
                for kind, ref in enumerate(sizes(g, core)):
                    for w in (0, 2):
                        rcopy(ref, ref, send_sem.at[g, kind + w], relay_recv.at[g, 0], sib).wait_send()

    def project(item, xb):
        part = jnp.dot(xv[:, KX * xb:KX * (xb + 1)], buf[item, xb].reshape(KX, F), preferred_element_type=F32)
        if xb == 0:
            acc[...] = part
        else:
            acc[...] += part

    def silu(v):
        return v * jax.nn.sigmoid(v)

    def local_state():
        for h in range(2):
            tail = jnp.exp((T - 1.0 - pos((T, HD), 0)) * log_decay[h])
            cols = pl.ds(HD * h, HD)
            kt = (kv[0, :, cols].astype(F32) * tail).astype(BF)
            state[h] = lax.dot_general(kt, kv[1, :, cols], (((0,), (0,)), ((), ())), preferred_element_type=F32)

    whole = lambda n: jnp.exp((n * T) * ld_mine)
    total = {}

    def scan_open():
        rcopy(state.at[1 - c], sx, st_send.at[0], st_recv.at[0], sib).start()

    def scan_chip():
        rcopy(state.at[1 - c], sx, st_send.at[0], st_recv.at[0], sib).wait_recv()
        mine, other = state[c], sx[...]
        decay = whole(1.0)
        first = jnp.where(c == 0, mine, other)
        second = jnp.where(c == 0, other, mine)
        total["first"] = first
        stg[0] = first
        tot = decay * first + second
        stg[1] = tot
        stg[2] = jnp.zeros_like(tot)
        snd[0] = tot.astype(BF)
        rcopy(snd.at[0], rcv.at[0], st_send.at[1], st_recv.at[1], partners[0]).start()

    def scan_step(k):
        rcopy(snd.at[k], rcv.at[k], st_send.at[1 + k], st_recv.at[1 + k], partners[k]).wait_recv()
        got = rcv[k].astype(F32)
        upper = (q // 2 ** k) % 2
        reach = (q % 2 ** k).astype(F32)
        span = whole(2.0 * 2 ** k)
        stg[2] += jnp.where(upper == 1, whole(2.0 * reach), 0.0) * got
        if k < 4:
            tot = stg[1]
            tot = jnp.where(upper == 1, tot + span * got, span * tot + got)
            stg[1] = tot
            snd[k + 1] = tot.astype(BF)
            rcopy(snd.at[k + 1], rcv.at[k + 1], st_send.at[2 + k], st_recv.at[2 + k], partners[k + 1]).start()
        else:
            low = stg[2]
            high = whole(1.0) * low + stg[0]
            pri[c] = jnp.where(c == 0, low, high)
            stg[3] = jnp.where(c == 0, high, low)
            rcopy(stg.at[3], pri.at[c], st_send.at[6], st_recv.at[6], sib).start()

    def scan_close():
        rcopy(stg.at[3], pri.at[1 - c], st_send.at[6], st_recv.at[6], sib).wait_recv()

    def intra(h, r):
        cols = pl.ds(HD * h, HD)
        rows = pl.ds(128 * r, 128)
        seen = 128 * (r + 1)
        scores = lax.dot_general(qv[rows, cols], kv[0, :seen, cols], (((1,), (1,)), ((), ())), preferred_element_type=F32)
        probs = (scores * wts[h, rows, :seen]).astype(BF)
        att[rows, cols] = jnp.dot(probs, kv[1, :seen, cols], preferred_element_type=F32)

    def inter(h):
        cols = pl.ds(HD * h, HD)
        into = jnp.exp((pos((T, HD), 0) + 1.0) * log_decay[h])
        prior = pri[h]
        top = prior.astype(BF)
        rest = (prior - top.astype(F32)).astype(BF)
        query = qv[:, cols]
        got = jnp.dot(query, top, preferred_element_type=F32) + jnp.dot(query, rest, preferred_element_type=F32)
        full = att[:, cols] + into * got
        scale = lax.rsqrt(jnp.mean(full * full, axis=1, keepdims=True) + 1e-06)
        att[:, cols] = full * scale * gain_ref[:, HD * h:HD * (h + 1)]

    def hcopy(src_y, r, lo, n, slot, device):
        ref = hid.at[src_y, pl.ds(128 * r + lo, n), :]
        return rcopy(ref, ref, h_send.at[r, slot], h_recv.at[r, slot], device)

    def gate(r):
        rows = pl.ds(128 * r, 128)
        hid[y, rows, :] = (att[rows, :] * jax.nn.sigmoid(acc[rows, :])).astype(BF)
        hcopy(y, r, 0, 128, 0, to_yp).start()
        hcopy(y, r, 0, 128, 1, to_ym).start()

    def forward(r):
        hcopy(ym, r, 0, 128, 0, to_yp).wait_recv()
        hcopy(ym, r, 0, 64, 2, to_yp).start()
        hcopy(yp, r, 0, 128, 1, to_ym).wait_recv()
        hcopy(yp, r, 64, 64, 3, to_ym).start()

    def far(r):
        hcopy(y2, r, 0, 64, 2, to_yp).wait_recv()
        hcopy(y2, r, 64, 64, 3, to_ym).wait_recv()

    def out_part(py, first, last):
        for j in range(6):
            cols = pl.ds(F * j, F)
            w = buf[4, py, :, :, 16 * j:16 * (j + 1), :].reshape(F, F)
            part = jnp.dot(hid[py], w, preferred_element_type=F32)
            if first:
                oacc[:, cols] = part
            elif not last:
                oacc[:, cols] += part
            else:
                outv[:, cols] = (oacc[:, cols] + part).astype(BF)
                pltpu.make_async_copy(outv.at[:, cols], out_hbm.at[:, cols], out_sem.at[j]).start()

    def take(index, fn):
        def run():
            fn(index)
        return run

    def finish_k():
        kv[0] = silu(acc[...]).astype(BF)

    def finish_v():
        kv[1] = silu(acc[...]).astype(BF)

    def finish_q():
        qv[...] = silu(acc[...]).astype(BF)

    P0 = functools.partial
    tasks = []
    for item, done in ((0, finish_k), (1, finish_v)):
        for xb in range(NX):
            tasks.append((0, 0.6, P0(project, item, xb)))
        tasks.append((0, 0.3, done))
    tasks.append((0, 0.5, local_state))
    tasks.append((0, 0.2, scan_open))
    tasks.append((0, 0.6, scan_chip))
    tasks.append((0, 1.2, P0(scan_step, 0)))
    tasks.append((0, 1.2, P0(scan_step, 1)))
    tasks.append((0, 1.2, P0(scan_step, 2)))
    for xb in range(NX):
        tasks.append((1, 0.6, P0(project, 2, xb)))
    tasks.append((1, 0.3, finish_q))
    tasks.append((1, 1.2, P0(scan_step, 3)))
    for r in range(2):
        for h in range(2):
            tasks.append((1, 0.3, P0(intra, h, r)))
    tasks.append((1, 1.2, P0(scan_step, 4)))
    for r in range(2, 4):
        for h in range(2):
            tasks.append((1, 0.3, P0(intra, h, r)))
    tasks.append((1, 0.6, scan_close))
    for h in range(2):
        tasks.append((1, 0.5, P0(inter, h)))
    for xb in range(NX):
        tasks.append((2, 0.6, P0(project, 3, xb)))
    for r in range(4):
        tasks.append((2, 0.2, P0(gate, r)))
    for r in range(4):
        tasks.append((2, 1.5, P0(forward, r)))

    whole_groups = set()
    asked = set()

    def run_tasks(budget):
        while tasks and budget > 0:
            group, cost, fn = tasks[0]
            if group not in whole_groups:
                return
            if group not in asked:
                asked.add(group)
                relays_arrived(group)
                if group == 0:
                    x_load.wait()
            tasks.pop(0)
            fn()
            budget -= cost

    for slot in range(max(OFFSETS) + STAGES):
        if slot == 1:
            lax.fori_loop(0, T // 64, table, 0)
        for g in range(len(GROUPS)):
            t = slot - OFFSETS[g]
            if 0 <= t < STAGES:
                stage(g, t)
                if t == STAGES - 1:
                    whole_groups.add(g)
                run_tasks(1.2)
    run_tasks(1000.0)
    relays_arrived(3)
    out_part(y, True, False)
    out_part(ym, False, False)
    out_part(yp, False, False)
    for r in range(4):
        far(r)
    out_part(y2, False, True)

    for g in range(len(GROUPS)):
        sends_done(g)
    rcopy(state.at[1 - c], sx, st_send.at[0], st_recv.at[0], sib).wait_send()
    for k in range(5):
        rcopy(snd.at[k], rcv.at[k], st_send.at[1 + k], st_recv.at[1 + k], partners[k]).wait_send()
    rcopy(stg.at[3], pri.at[c], st_send.at[6], st_recv.at[6], sib).wait_send()
    for r in range(4):
        hcopy(y, r, 0, 128, 0, to_yp).wait_send()
        hcopy(y, r, 0, 128, 1, to_ym).wait_send()
        hcopy(ym, r, 0, 64, 2, to_yp).wait_send()
        hcopy(yp, r, 64, 64, 3, to_ym).wait_send()
    for j in range(6):
        cols = pl.ds(F * j, F)
        pltpu.make_async_copy(outv.at[:, cols], out_hbm.at[:, cols], out_sem.at[j]).wait()


def shards(inputs, proj_weight, decay_codes, norm_gain, out_weight):
    vmem = pltpu.VMEM
    dma = pltpu.SemaphoreType.DMA
    hbm = pl.BlockSpec(memory_space=pl.ANY)
    ng = len(GROUPS)
    return pl.pallas_call(
        kernel,
        out_shape=jax.ShapeDtypeStruct((T, 1536), BF),
        in_specs=[hbm, hbm, pl.BlockSpec(memory_space=pltpu.SMEM), pl.BlockSpec(memory_space=vmem), hbm],
        out_specs=hbm,
        scratch_shapes=[
            vmem((5, NX, NZ, 2, SH, F), BF),
            vmem((T, D), BF),
            vmem((2, T, T), F32),
            vmem((T, F), F32),
            vmem((2, T, F), BF),
            vmem((T, F), BF),
            vmem((T, F), F32),
            vmem((NY, T, F), BF),
            vmem((T, 1536), F32),
            vmem((T, 1536), BF),
            vmem((2, HD, HD), F32),
            vmem((HD, HD), F32),
            vmem((5, HD, HD), BF),
            vmem((5, HD, HD), BF),
            vmem((4, HD, HD), F32),
            vmem((2, HD, HD), F32),
            dma((10,)),
            dma((ng,)),
            dma((ng,)),
            dma((ng, NSLOT)),
            dma((ng, 2)),
            dma((ng, 4)),
            dma((7,)),
            dma((7,)),
            dma((4, 4)),
            dma((4, 4)),
            dma((6,)),
        ],
        compiler_params=pltpu.CompilerParams(collective_id=0, has_side_effects=True, vmem_limit_bytes=56 * 2 ** 20),
        name="lightning",
    )(inputs, proj_weight, decay_codes, norm_gain.reshape(1, F), out_weight)


def solution(mesh):
    in_specs = (P("seq", None), P(None, "seq", "tp"), P("tp"), P("tp"), P("seq", "tp"))
    out_specs = P("seq", "tp")
    return jax.shard_map(shards, mesh=mesh, in_specs=in_specs, out_specs=out_specs, check_vma=False)
```

```python
import functools

import jax
import jax.numpy as jnp
from jax import lax
from jax.experimental import pallas as pl
from jax.experimental.pallas import tpu as pltpu
from jax.sharding import PartitionSpec as P

NX, NZ, NY = 4, 8, 4
T = 512
D = 6144
HD = 128
F = 256
SH = 96
KX = D // NX
MESH = pl.DeviceIdType.MESH
BF = jnp.bfloat16
F32 = jnp.float32

NSLOT = 40

GROUPS = ((0, 2, 32), (2, 1, 48), (3, 1, 32), (4, 1, 32))
PLAN = (
    ("table", ((0, -1),),
     ((0, -1),)),
    ("K0", ((0, 0), (0, 1), (0, 4), (0, 5), (0, 2), (0, 12), (0, 13), (0, 20), (0, 21), (0, 6), (0, 7), (0, 28), (0, 29), (0, 14), (0, 15), (0, 22), (0, 23), (0, 8), (1, -1), (0, 9), (0, 30), (0, 31), (0, 16), (0, 17), (1, 0), (1, 1), (0, 24), (0, 25), (0, 10), (1, 2), (1, 5), (1, 4), (2, -1), (0, 11), (0, 32), (0, 33), (0, 18), (0, 19), (1, 12), (1, 13), (1, 20), (1, 21), (0, 26), (0, 27), (1, 28), (1, 29), (1, 6), (1, 7), (2, 4), (2, 5), (0, 34), (0, 35), (1, 14), (1, 15), (1, 22), (1, 23), (2, 0), (2, 1), (1, 30), (2, 2), (1, 31), (1, 8), (1, 9), (2, 6), (2, 7), (3, -1), (1, 16), (1, 17), (1, 24), (1, 25), (2, 12), (2, 13), (2, 20), (2, 21), (2, 29),),
     ((0, 0), (0, 1), (0, 8), (0, 9), (0, 12), (0, 13), (0, 2), (0, 3), (0, 16), (0, 17), (0, 10), (0, 11), (0, 14), (0, 15), (1, -1), (0, 20), (0, 21), (0, 4), (0, 5), (0, 24), (0, 25), (0, 18), (0, 19), (0, 6), (0, 7), (1, 8), (1, 9), (1, 1), (1, 0), (0, 22), (0, 23), (2, -1), (0, 28), (0, 29), (0, 32), (0, 33), (1, 3), (0, 26), (0, 27), (1, 2), (0, 36), (0, 37), (2, 0), (1, 10), (2, 1), (1, 11), (1, 16), (1, 17), (1, 12), (1, 13), (2, 8), (2, 9), (1, 5), (1, 4), (0, 30), (0, 31), (1, 7), (1, 6), (0, 34), (0, 35), (1, 24), (1, 25), (2, 2), (2, 3), (1, 20), (3, -1), (1, 21), (0, 38), (0, 39),)),
    ("K1", ((1, 32), (2, 28), (1, 33), (1, 10), (1, 11),),
     ()),
    ("K2", (),
     ((2, 12), (2, 13),)),
    ("K3", (),
     ((2, 16), (2, 17), (1, 18), (1, 19), (1, 14), (1, 15),)),
    ("finK", (),
     ((2, 10), (2, 11),)),
    ("V0", (),
     ((1, 32), (1, 33), (2, 4), (2, 5),)),
    ("V1", ((2, 8), (2, 9),),
     ((1, 28), (1, 29), (1, 36), (1, 37), (2, 6), (2, 7), (1, 26), (1, 27),)),
    ("V2", (),
     ((3, 0), (3, 1), (2, 20), (2, 21),)),
    ("V3", ((3, 4), (3, 5), (1, 18), (1, 19), (1, 26), (1, 27),),
     ((2, 24), (2, 25), (1, 22),)),
    ("finV", ((2, 14), (2, 15), (2, 22), (2, 23), (1, 34), (2, 31), (3, 1), (2, 30), (3, 0), (1, 35), (2, 10), (2, 11),),
     ((3, 9), (3, 8),)),
    ("state", (),
     ()),
    ("chip", ((3, 2), (3, 6), (3, 7),),
     ((1, 23), (2, 14), (2, 15), (3, 2), (2, 18), (2, 19), (3, 3), (1, 34), (1, 35), (2, 28), (2, 29),)),
    ("Q0", ((2, 16), (2, 17), (2, 24), (2, 25), (3, 20), (2, 33), (2, 32), (3, 21), (3, 12), (3, 13), (3, 29),),
     ((2, 32), (2, 33), (1, 30), (1, 31), (1, 38), (1, 39),)),
    ("Q1", ((3, 28),),
     ()),
    ("st0", ((3, 8), (3, 9), (2, 18), (2, 19), (2, 26),),
     ((3, 4), (2, 36), (2, 37), (3, 5), (3, 12), (3, 13), (3, 6), (3, 16), (3, 17), (3, 7), (2, 22), (2, 23),)),
    ("Q2", ((2, 27),),
     ((2, 26), (2, 27),)),
    ("Q3", ((2, 35), (3, 22), (2, 34), (3, 23), (3, 14), (3, 15),),
     ((3, 10), (3, 11),)),
    ("finQ", ((3, 31), (3, 30),),
     ((3, 20), (3, 21),)),
    ("intra0", ((3, 10), (3, 11),),
     ()),
    ("intra1", (),
     ((3, 24), (3, 25), (2, 30), (2, 31), (2, 34), (2, 35),)),
    ("st1", ((3, 24), (3, 25),),
     ((3, 28), (3, 29), (2, 38), (2, 39),)),
    ("G0", ((3, 16), (3, 17),),
     ((3, 32), (3, 33),)),
    ("G1", ((3, 33), (3, 32),),
     ((3, 14), (3, 15), (3, 18), (3, 19),)),
    ("G2", (),
     ((3, 36), (3, 37),)),
    ("G3", (),
     ((3, 22), (3, 23), (3, 26), (3, 27),)),
    ("st2", ((3, 26), (3, 27), (3, 18), (3, 19), (3, 35), (3, 34),),
     ((3, 30), (3, 31), (3, 34), (3, 35),)),
    ("inter", (),
     ((3, 38), (3, 39),)),
    ("gate0", (),
     ()),
    ("gate1", (),
     ()),
    ("gate2", (),
     ()),
    ("gate3", (),
     ()),
)


def kernel(x_hbm, wp_hbm, codes_hbm, gain_hbm, wo_hbm, out_hbm,
           codes, gain_ref, buf, xv, wts, acc, kv, qv, att, hid, oacc, outv,
           state, sx, snd, rcv, stg, pri,
           load_sem, own_send, own_recv, recv, relay_recv, send_sem,
           st_send, st_recv, h_send, h_recv, out_sem):
    s = lax.axis_index("seq")
    y = lax.axis_index("tp")
    x, z, c = s // 16, (s // 2) % 8, s % 2
    q = s // 2

    def dev(px, pz, pc, py):
        return {"seq": (px * NZ + pz) * 2 + pc, "tp": py}

    xp, xm = (x + 1) % NX, (x + 3) % NX
    zp, zm = (z + 1) % NZ, (z + 7) % NZ
    yp, ym = (y + 1) % NY, (y + 3) % NY
    x2, z4, y2 = (x + 2) % NX, (z + 4) % NZ, (y + 2) % NY
    sib = dev(x, z, 1 - c, y)
    zp2, zm2 = (z + 2) % NZ, (z + 6) % NZ
    to = {"xp": dev(xp, z, c, y), "xm": dev(xm, z, c, y), "zp": dev(x, zp, c, y), "zm": dev(x, zm, c, y),
          "x2": dev(x2, z, c, y), "zp2": dev(x, zp2, c, y), "zm2": dev(x, zm2, c, y)}
    to_y = (dev(x, z, c, yp), dev(x, z, c, ym), dev(x, z, c, y2))
    z_pair = dev(x, z + 1 - 2 * (z % 2), c, y)
    z_four = (to["zp2"], dev(x, z4, c, y), to["zm2"])
    x_four = (to["xp"], to["x2"], to["xm"])

    x_load = pltpu.make_async_copy(x_hbm, xv, load_sem.at[0])
    loads = [
        [pltpu.make_async_copy(wp_hbm.at[pl.ds(1, 2)], buf.at[pl.ds(0, 2), x, z, c], load_sem.at[1])],
        [pltpu.make_async_copy(wp_hbm.at[pl.ds(0, 1)], buf.at[pl.ds(2, 1), x, z, c], load_sem.at[2])],
        [pltpu.make_async_copy(wp_hbm.at[pl.ds(3, 1)], buf.at[pl.ds(3, 1), x, z, c], load_sem.at[3])],
        [pltpu.make_async_copy(wo_hbm.at[:, pl.ds(F * j, F)], buf.at[4, x, z, c, pl.ds(16 * j, 16), :], load_sem.at[4 + j])
         for j in range(6)],
    ]
    for group in loads:
        for copy in group:
            copy.start()
    small = [pltpu.make_async_copy(codes_hbm, codes, load_sem.at[10]),
             pltpu.make_async_copy(gain_hbm, gain_ref, load_sem.at[11])]
    for copy in small:
        copy.start()
    x_load.start()

    barrier = pltpu.get_barrier_semaphore()
    greet = list(to.values()) + [sib, z_four[1]] + list(to_y)
    for other in greet:
        pl.semaphore_signal(barrier, inc=1, device_id=other, device_id_type=MESH)
    pl.semaphore_wait(barrier, len(greet))

    def rcopy(src, dst, ssem, rsem, device):
        return pltpu.make_async_remote_copy(src, dst, ssem, rsem, device_id=device, device_id_type=MESH)

    def own_copy(g):
        i0, n, _ = GROUPS[g]
        ref = buf.at[pl.ds(i0, n), x, z, c]
        return rcopy(ref, ref, own_send.at[g], own_recv.at[g], sib)

    for g in range(len(GROUPS)):
        for copy in loads[g]:
            copy.wait()
        own_copy(g).start()

    for copy in small:
        copy.wait()
    pos = lambda shape, dim: lax.broadcasted_iota(jnp.int32, shape, dim).astype(F32)
    log_decay = [jnp.log1p(-(jnp.full((1, HD), codes[h], jnp.int32).astype(F32)) * 1e-06) for h in range(2)]
    ld_mine = jnp.where(c == 0, log_decay[0], log_decay[1])

    def table(r, carry):
        row = pos((64, T), 0) + (r * 64).astype(F32)
        diff = row - pos((64, T), 1)
        for h in range(2):
            ld = jnp.concatenate([log_decay[h]] * (T // HD), axis=1)
            w = jnp.where(diff >= 0, jnp.exp(jnp.maximum(diff, 0.0) * ld), 0.0)
            wts[h, pl.ds(pl.multiple_of(r * 64, 64), 64), :] = w
        return carry

    def piece(g, px, pz, rows, half=None):
        i0, n, _ = GROUPS[g]
        cc = pl.ds(0, 2) if half is None else pl.ds(half, 1)
        return buf.at[pl.ds(i0, n), px, pz, cc, pl.ds(*rows), :]

    def send(g, kind, ref, slot, where):
        rcopy(ref, ref, send_sem.at[g, kind], recv.at[g, slot], to[where]).start()

    def arrived(g, ref, slot):
        rcopy(ref, ref, send_sem.at[g, 0], recv.at[g, slot], sib).wait_recv()

    def relay(g, kind, ref):
        rcopy(ref, ref, send_sem.at[g, 2 + kind], relay_recv.at[g, kind], sib).start()

    def event_a(g, slot):
        pc = functools.partial(piece, g, rows=(0, GROUPS[g][2]))
        chain = lambda k, hop, way: 4 + (k * 4 + hop) * 2 + way
        columns = (x, xm, xp, x2)
        if slot < 3:
            k = slot + 1
            ref = pc(columns[k], z)
            if slot >= 0:
                arrived(g, ref, slot)
            else:
                for o, where in enumerate(("xp", "xm", "x2")):
                    send(g, 0, ref, o, where)
            send(g, 1, ref, chain(k, 0, 0), "zp")
            send(g, 1, ref, chain(k, 0, 1), "zm")
            if slot >= 0:
                relay(g, 0, ref)
            return
        k, hop, way = (slot - 4) // 8, (slot - 4) // 2 % 4, slot % 2
        pz = (z + (8 - hop - 1 if way == 0 else hop + 1)) % NZ
        ref = pc(columns[k], pz, half=way if hop == 3 else None)
        arrived(g, ref, slot)
        if hop < 3:
            part = pc(columns[k], pz, half=way if hop == 2 else None)
            send(g, 1, part, chain(k, hop + 1, way), ("zp", "zm")[way])
        relay(g, 1, ref)

    def event_b(g, slot, last):
        _, _, a = GROUPS[g]
        pc = functools.partial(piece, g, rows=(a, SH - a))
        zs = (0, -1, 1, -2, 2, -3, 3, 4)

        def across(k):
            ref = pc(x, (z + 8 + zs[k]) % NZ)
            send(g, 1, ref, 8 + 4 * k, "xp")
            send(g, 1, ref, 9 + 4 * k, "xm")

        if slot < 0:
            send(g, 0, pc(x, z), 0, "zp")
            send(g, 0, pc(x, z), 1, "zm")
            across(0)
        elif slot < 6:
            ref = pc(x, (z + 8 + zs[slot + 1]) % NZ)
            arrived(g, ref, slot)
            if slot < 4:
                send(g, 0, ref, slot + 2, ("zp", "zm")[slot % 2])
            if slot in (2, 3):
                half = pc(x, (z + 8 + zs[slot + 1]) % NZ, half=slot - 2)
                send(g, 0, half, slot + 4, ("zp2", "zm2")[slot - 2])
            across(slot + 1)
            relay(g, 0, ref)
        elif slot < 8:
            ref = pc(x, z4, half=slot - 6)
            arrived(g, ref, slot)
            relay(g, 0, ref)
            if last:
                across(7)
        else:
            k, j = (slot - 8) // 4, slot % 4
            pz = (z + 8 + zs[k]) % NZ
            ref = pc((xm, xp, x2, x2)[j], pz, half=None if j < 2 else j - 2)
            arrived(g, ref, slot)
            if j < 2:
                send(g, 1, pc((xm, xp)[j], pz, half=j), slot + 2, ("xp", "xm")[j])
            relay(g, 1, ref)

    def events(core, todo, seen):
        for g, slot in todo:
            if slot < 0:
                i0, n, _ = GROUPS[g]
                ref = buf.at[pl.ds(i0, n), x, z, 1 - c]
                rcopy(ref, ref, own_send.at[g], own_recv.at[g], sib).wait_recv()
            if core == 0:
                event_a(g, slot)
            else:
                event_b(g, slot, (g, 13 - slot) in seen)
            seen.add((g, slot))

    def sizes(g, core):
        i0, n, a = GROUPS[g]
        if core == 0:
            return [buf.at[pl.ds(i0, n), pl.ds(0, 3), 0, :, pl.ds(0, a), :],
                    buf.at[pl.ds(i0, n), :, pl.ds(0, 7), :, pl.ds(0, a), :]]
        return [buf.at[pl.ds(i0, n), 0, pl.ds(0, 7), :, pl.ds(a, SH - a), :],
                buf.at[pl.ds(i0, n), pl.ds(0, 3), :, :, pl.ds(a, SH - a), :]]

    def relays_arrived(g):
        for core in range(2):
            @pl.when(c == 1 - core)
            def _(core=core):
                for kind, ref in enumerate(sizes(g, core)):
                    rcopy(ref, ref, send_sem.at[g, 0], relay_recv.at[g, kind], sib).wait_recv()

    def sends_done(g):
        own_copy(g).wait_send()
        for core in range(2):
            @pl.when(c == core)
            def _(core=core):
                for kind, ref in enumerate(sizes(g, core)):
                    for w in (0, 2):
                        rcopy(ref, ref, send_sem.at[g, kind + w], relay_recv.at[g, 0], sib).wait_send()

    def project(item, xb):
        part = jnp.dot(xv[:, KX * xb:KX * (xb + 1)], buf[item, xb].reshape(KX, F), preferred_element_type=F32)
        if xb == 0:
            acc[...] = part
        else:
            acc[...] += part

    def silu(v):
        return v * jax.nn.sigmoid(v)

    def local_state():
        for h in range(2):
            tail = jnp.exp((T - 1.0 - pos((T, HD), 0)) * log_decay[h])
            cols = pl.ds(HD * h, HD)
            kt = (kv[0, :, cols].astype(F32) * tail).astype(BF)
            state[h] = lax.dot_general(kt, kv[1, :, cols], (((0,), (0,)), ((), ())), preferred_element_type=F32)

    whole = lambda n: jnp.exp((n * T) * ld_mine)

    def scan_open():
        rcopy(state.at[1 - c], sx, st_send.at[0, 0], st_recv.at[0, 0], sib).start()

    def scan_chip():
        rcopy(state.at[1 - c], sx, st_send.at[0, 0], st_recv.at[0, 0], sib).wait_recv()
        mine, other = state[c], sx[...]
        first = jnp.where(c == 0, mine, other)
        stg[0] = first
        stg[1] = whole(1.0) * first + jnp.where(c == 0, other, mine)
        stg[2] = jnp.zeros_like(first)

    steps = (((z_pair,), z % 2, 1, 0), (z_four, z // 2, 2, z % 2), (x_four, x, 8, z))

    def scan_send(k):
        snd[k] = stg[1].astype(BF)
        for o, other in enumerate(steps[k][0]):
            rcopy(snd.at[k], rcv.at[k, o], st_send.at[1 + k, o], st_recv.at[1 + k, o], other).start()

    def scan_step(k):
        others, place, span, reach = steps[k]
        count = len(others) + 1
        chips = lambda n: whole(2.0 * jnp.asarray(n, jnp.int32).astype(F32))
        tot = stg[1] * chips((count - 1 - place) * span)
        before = stg[2]
        for o, other in enumerate(others):
            rcopy(snd.at[k], rcv.at[k, o], st_send.at[1 + k, o], st_recv.at[1 + k, o], other).wait_recv()
            got = rcv[k, o].astype(F32)
            source = (place + count - 1 - o) % count
            before += jnp.where(place > o, chips(o * span + reach), 0.0) * got
            tot += chips((count - 1 - source) * span) * got
        stg[1] = tot
        stg[2] = before

    def scan_end():
        low = stg[2]
        high = whole(1.0) * low + stg[0]
        pri[c] = jnp.where(c == 0, low, high)
        stg[3] = jnp.where(c == 0, high, low)
        rcopy(stg.at[3], pri.at[c], st_send.at[0, 1], st_recv.at[0, 1], sib).start()

    def scan_close():
        rcopy(stg.at[3], pri.at[1 - c], st_send.at[0, 1], st_recv.at[0, 1], sib).wait_recv()

    def intra(h, r):
        cols = pl.ds(HD * h, HD)
        rows = pl.ds(128 * r, 128)
        seen = 128 * (r + 1)
        scores = lax.dot_general(qv[rows, cols], kv[0, :seen, cols], (((1,), (1,)), ((), ())), preferred_element_type=F32)
        probs = (scores * wts[h, rows, :seen]).astype(BF)
        att[rows, cols] = jnp.dot(probs, kv[1, :seen, cols], preferred_element_type=F32)

    def inter(h):
        cols = pl.ds(HD * h, HD)
        into = jnp.exp((pos((T, HD), 0) + 1.0) * log_decay[h])
        prior = pri[h]
        top = prior.astype(BF)
        rest = (prior - top.astype(F32)).astype(BF)
        query = qv[:, cols]
        got = jnp.dot(query, top, preferred_element_type=F32) + jnp.dot(query, rest, preferred_element_type=F32)
        full = att[:, cols] + into * got
        scale = lax.rsqrt(jnp.mean(full * full, axis=1, keepdims=True) + 1e-06)
        att[:, cols] = full * scale * gain_ref[:, HD * h:HD * (h + 1)]

    def hcopy(src_y, r, slot, device):
        ref = hid.at[src_y, pl.ds(128 * r, 128), :]
        return rcopy(ref, ref, h_send.at[r, slot], h_recv.at[r, slot], device)

    def gate(r):
        rows = pl.ds(128 * r, 128)
        hid[y, rows, :] = (att[rows, :] * jax.nn.sigmoid(acc[rows, :])).astype(BF)
        for o in range(3):
            hcopy(y, r, o, to_y[o]).start()

    def heads_arrived(o):
        for r in range(4):
            hcopy((ym, yp, y2)[o], r, o, to_y[o]).wait_recv()

    def out_part(py, first, last):
        for j in range(6):
            cols = pl.ds(F * j, F)
            w = buf[4, py, :, :, 16 * j:16 * (j + 1), :].reshape(F, F)
            part = jnp.dot(hid[py], w, preferred_element_type=F32)
            if first:
                oacc[:, cols] = part
            elif not last:
                oacc[:, cols] += part
            else:
                outv[:, cols] = (oacc[:, cols] + part).astype(BF)
                pltpu.make_async_copy(outv.at[:, cols], out_hbm.at[:, cols], out_sem.at[j]).start()

    def finish_k():
        kv[0] = silu(acc[...]).astype(BF)

    def finish_v():
        kv[1] = silu(acc[...]).astype(BF)

    def finish_q():
        qv[...] = silu(acc[...]).astype(BF)

    def weights(g):
        relays_arrived(g)
        if g == 0:
            x_load.wait()

    def project_all(item):
        for xb in range(NX):
            project(item, xb)

    def act(name):
        kind, n = name.rstrip("0123"), name[-1]
        n = int(n) if n.isdigit() else None
        if kind == "table":
            lax.fori_loop(0, T // 64, table, 0)
        elif kind in "KVQG":
            item = "KVQG".index(kind)
            if n == 0 and kind != "V":
                weights((0, 0, 1, 2)[item])
            project(item, n)
        elif kind == "fin" + name[-1]:
            (finish_k if n is None and name[-1] == "K" else finish_v if name[-1] == "V" else finish_q)()
        elif kind == "state":
            local_state()
            scan_open()
        elif kind == "chip":
            scan_chip()
            scan_send(0)
        elif kind == "st":
            scan_step(n)
            if n < 2:
                scan_send(n + 1)
            else:
                scan_end()
        elif kind == "intra":
            for r in range(4):
                intra(n, r)
        elif kind == "inter":
            scan_close()
            for h in range(2):
                inter(h)
        elif kind == "gate":
            gate(n)

    seen = (set(), set())
    for name, *todo in PLAN:
        for core in range(2):
            if todo[core]:
                @pl.when(c == core)
                def _(core=core, todo=todo):
                    events(core, todo[core], seen[core])
        if name:
            act(name)

    weights(3)
    out_part(y, True, False)
    heads_arrived(0)
    out_part(ym, False, False)
    heads_arrived(1)
    out_part(yp, False, False)
    heads_arrived(2)
    out_part(y2, False, True)

    for g in range(len(GROUPS)):
        sends_done(g)
    rcopy(state.at[1 - c], sx, st_send.at[0, 0], st_recv.at[0, 0], sib).wait_send()
    rcopy(stg.at[3], pri.at[c], st_send.at[0, 1], st_recv.at[0, 1], sib).wait_send()
    for k in range(3):
        for o, other in enumerate(steps[k][0]):
            rcopy(snd.at[k], rcv.at[k, o], st_send.at[1 + k, o], st_recv.at[1 + k, o], other).wait_send()
    for r in range(4):
        for o in range(3):
            hcopy(y, r, o, to_y[o]).wait_send()
    for j in range(6):
        cols = pl.ds(F * j, F)
        pltpu.make_async_copy(outv.at[:, cols], out_hbm.at[:, cols], out_sem.at[j]).wait()


def shards(inputs, proj_weight, decay_codes, norm_gain, out_weight):
    vmem = pltpu.VMEM
    dma = pltpu.SemaphoreType.DMA
    hbm = pl.BlockSpec(memory_space=pltpu.HBM)
    ng = len(GROUPS)
    args = (inputs, proj_weight, decay_codes, norm_gain.reshape(1, F), out_weight)
    args = [pltpu.with_memory_space_constraint(a, pltpu.HBM) for a in args]
    return pl.pallas_call(
        kernel,
        out_shape=jax.ShapeDtypeStruct((T, 1536), BF),
        in_specs=[hbm] * 5,
        out_specs=pl.BlockSpec(memory_space=pl.ANY),
        scratch_shapes=[
            pltpu.SMEM((2,), jnp.int32),
            vmem((1, F), F32),
            vmem((5, NX, NZ, 2, SH, F), BF),
            vmem((T, D), BF),
            vmem((2, T, T), F32),
            vmem((T, F), F32),
            vmem((2, T, F), BF),
            vmem((T, F), BF),
            vmem((T, F), F32),
            vmem((NY, T, F), BF),
            vmem((T, 1536), F32),
            vmem((T, 1536), BF),
            vmem((2, HD, HD), F32),
            vmem((HD, HD), F32),
            vmem((3, HD, HD), BF),
            vmem((3, 3, HD, HD), BF),
            vmem((4, HD, HD), F32),
            vmem((2, HD, HD), F32),
            dma((12,)),
            dma((ng,)),
            dma((ng,)),
            dma((ng, NSLOT)),
            dma((ng, 2)),
            dma((ng, 4)),
            dma((4, 3)),
            dma((4, 3)),
            dma((4, 3)),
            dma((4, 3)),
            dma((6,)),
        ],
        compiler_params=pltpu.CompilerParams(collective_id=0, has_side_effects=True, vmem_limit_bytes=52 * 2 ** 20),
        name="lightning",
    )(*args)


def solution(mesh):
    in_specs = (P("seq", None), P(None, "seq", "tp"), P("tp"), P("tp"), P("seq", "tp"))
    out_specs = P("seq", "tp")
    return jax.shard_map(shards, mesh=mesh, in_specs=in_specs, out_specs=out_specs, check_vma=False)
```

```python
import functools

import jax
import jax.numpy as jnp
from jax import lax
from jax.experimental import pallas as pl
from jax.experimental.pallas import tpu as pltpu
from jax.sharding import PartitionSpec as P

NX, NZ, NY = 4, 8, 4
T = 512
D = 6144
HD = 128
F = 256
SH = 96
KX = D // NX
MESH = pl.DeviceIdType.MESH
BF = jnp.bfloat16
F32 = jnp.float32

NSLOT = 40

GROUPS = ((0, 2, 32), (2, 1, 32), (3, 1, 48), (4, 1, 48))
PLAN = (
    ("table", ((0, -1),),
     ((0, -1),)),
    ("K0", ((0, 0), (0, 1), (0, 4), (0, 5), (0, 2), (0, 12), (0, 13), (0, 20), (0, 21), (0, 6), (0, 7), (0, 28), (0, 29), (1, -1), (0, 14), (0, 15), (0, 22), (0, 23), (0, 8), (0, 9), (0, 30), (0, 31), (1, 4), (1, 5), (1, 0), (1, 1), (1, 2), (0, 16), (0, 17), (2, -1), (0, 24), (0, 25), (0, 10), (0, 11),),
     ((0, 0), (0, 1), (0, 8), (0, 9), (0, 12), (0, 13), (0, 2), (0, 3), (0, 16), (0, 17), (1, -1), (0, 10), (0, 11), (0, 14), (0, 15), (0, 20), (0, 21), (0, 4), (0, 5), (0, 24), (0, 25), (0, 18), (0, 19), (0, 6), (0, 7), (1, 0), (1, 1), (1, 8), (1, 9), (2, -1), (0, 22), (0, 23), (0, 28), (0, 29),)),
    ("V0", (),
     ()),
    ("K1", ((0, 32), (0, 33), (1, 6), (1, 7), (1, 12), (1, 13), (1, 20), (1, 21), (1, 28), (1, 29), (0, 18), (0, 19), (2, 4), (2, 5), (0, 26), (0, 27), (0, 34), (0, 35), (1, 8), (1, 9), (1, 14), (1, 15),),
     ((0, 32), (0, 33), (1, 2), (1, 3), (0, 26), (0, 27), (2, 1), (2, 0), (0, 36), (0, 37), (1, 12), (1, 13),)),
    ("K2", ((3, -1), (1, 22), (1, 23),),
     ((1, 16), (1, 17),)),
    ("V1", ((2, 0), (2, 1),),
     ((3, -1), (1, 10), (1, 11), (2, 8), (2, 9), (1, 4), (1, 5),)),
    ("V2", ((1, 30), (1, 31),),
     ()),
    ("Q0", ((2, 2), (2, 6), (2, 7), (1, 10), (1, 11), (1, 16), (1, 17),),
     ((1, 6), (1, 7), (2, 2), (2, 3), (0, 30), (0, 31), (0, 34), (0, 35), (1, 20), (1, 21),)),
    ("K3", ((3, 4), (3, 5), (1, 24), (1, 25), (2, 12), (2, 13), (2, 20), (2, 21), (1, 32), (1, 33), (2, 29), (3, 0), (3, 1), (2, 28),),
     ((3, 0), (3, 1), (1, 24), (1, 25), (2, 16), (2, 17), (2, 12), (2, 13), (0, 38), (0, 39),)),
    ("V3", ((2, 8), (2, 9), (1, 18), (1, 19), (3, 2),),
     ((1, 14), (1, 15), (2, 4), (1, 18), (1, 19), (2, 5),)),
    ("finK", ((3, 6), (3, 7), (1, 26), (1, 27),),
     ((2, 6),)),
    ("finV", (),
     ()),
    ("state", (),
     ()),
    ("chip", ((2, 14), (2, 15),),
     ((2, 7), (3, 8), (3, 9), (2, 10), (2, 11), (1, 28), (1, 29), (3, 2), (3, 3), (1, 32), (1, 33), (1, 36), (1, 37), (2, 20), (2, 21),)),
    ("Q1", ((2, 22), (2, 23), (1, 34), (1, 35), (3, 12), (2, 31), (3, 20), (3, 13),),
     ()),
    ("Q2", ((2, 30), (3, 21), (2, 10), (2, 11),),
     ((2, 24), (2, 25), (1, 22), (1, 23),)),
    ("G0", ((3, 28), (3, 29),),
     ((3, 12), (3, 13), (3, 16), (3, 17), (1, 26), (1, 27), (2, 18), (2, 19), (2, 14), (2, 15), (3, 4), (3, 5),)),
    ("st0", ((3, 8), (3, 9), (2, 16), (2, 17),),
     ((2, 28), (2, 29), (2, 32), (2, 33), (3, 6), (3, 7), (2, 36), (2, 37), (3, 10), (3, 11), (1, 30), (1, 31),)),
    ("G1", ((2, 24), (2, 25), (3, 14), (2, 33), (3, 22), (3, 15), (2, 32), (3, 23), (3, 30), (3, 31), (3, 10), (3, 11), (2, 18), (2, 19),),
     ((3, 20), (3, 21), (3, 24), (3, 25), (1, 34), (1, 35), (1, 38), (1, 39), (2, 22), (2, 23), (2, 26), (2, 27), (3, 14), (3, 15), (3, 18), (3, 19), (3, 28), (3, 29),)),
    ("Q3", (),
     ((3, 32), (3, 33), (2, 30), (2, 31), (2, 34), (2, 35),)),
    ("finQ", (),
     ((3, 36), (3, 37), (2, 38), (2, 39), (3, 22), (3, 23), (3, 26), (3, 27),)),
    ("intra0", (),
     ((3, 30), (3, 31),)),
    ("intra1", ((2, 26), (2, 27),),
     ((3, 34),)),
    ("st1", ((2, 35), (3, 16),),
     ((3, 35),)),
    ("G2", (),
     ()),
    ("G3", ((3, 17), (3, 24), (2, 34), (3, 25),),
     ()),
    ("st2", ((3, 32), (3, 33), (3, 18),),
     ((3, 38), (3, 39),)),
    ("inter", ((3, 19), (3, 26), (3, 27), (3, 34), (3, 35),),
     ()),
    ("gate0", (),
     ()),
    ("gate1", (),
     ()),
    ("gate2", (),
     ()),
    ("gate3", (),
     ()),
    ("out0", (),
     ()),
    ("fwd0", (),
     ()),
    ("fwd1", (),
     ()),
    ("fwd2", (),
     ()),
    ("fwd3", (),
     ()),
    ("out1", (),
     ()),
    ("out2", (),
     ()),
    ("out3", (),
     ()),
)


def kernel(x_hbm, wp_hbm, codes_hbm, gain_hbm, wo_hbm, out_hbm,
           codes, gain_ref, buf, xv, wts, acc, kv, qv, att, hid, oacc, outv,
           state, sx, snd, rcv, stg, pri,
           load_sem, own_send, own_recv, recv, relay_recv, relay_send, send_sem,
           st_send, st_recv, h_send, h_recv, out_sem):
    s = lax.axis_index("seq")
    y = lax.axis_index("tp")
    x, z, c = s // 16, (s // 2) % 8, s % 2
    q = s // 2

    def dev(px, pz, pc, py):
        return {"seq": (px * NZ + pz) * 2 + pc, "tp": py}

    xp, xm = (x + 1) % NX, (x + 3) % NX
    zp, zm = (z + 1) % NZ, (z + 7) % NZ
    yp, ym = (y + 1) % NY, (y + 3) % NY
    x2, z4, y2 = (x + 2) % NX, (z + 4) % NZ, (y + 2) % NY
    sib = dev(x, z, 1 - c, y)
    zp2, zm2 = (z + 2) % NZ, (z + 6) % NZ
    to = {"xp": dev(xp, z, c, y), "xm": dev(xm, z, c, y), "zp": dev(x, zp, c, y), "zm": dev(x, zm, c, y),
          "x2": dev(x2, z, c, y), "zp2": dev(x, zp2, c, y), "zm2": dev(x, zm2, c, y)}
    to_y = (dev(x, z, c, yp), dev(x, z, c, ym))
    z_pair = dev(x, z + 1 - 2 * (z % 2), c, y)
    z_four = (to["zp2"], dev(x, z4, c, y), to["zm2"])
    x_four = (to["xp"], to["x2"], to["xm"])

    x_load = pltpu.make_async_copy(x_hbm, xv, load_sem.at[0])
    loads = [
        [pltpu.make_async_copy(wp_hbm.at[pl.ds(1, 2)], buf.at[pl.ds(0, 2), x, z, c], load_sem.at[1])],
        [pltpu.make_async_copy(wp_hbm.at[pl.ds(0, 1)], buf.at[pl.ds(2, 1), x, z, c], load_sem.at[2])],
        [pltpu.make_async_copy(wp_hbm.at[pl.ds(3, 1)], buf.at[pl.ds(3, 1), x, z, c], load_sem.at[3])],
        [pltpu.make_async_copy(wo_hbm.at[:, pl.ds(F * j, F)], buf.at[4, x, z, c, pl.ds(16 * j, 16), :], load_sem.at[4 + j])
         for j in range(6)],
    ]
    for group in loads:
        for copy in group:
            copy.start()
    small = [pltpu.make_async_copy(codes_hbm, codes, load_sem.at[10]),
             pltpu.make_async_copy(gain_hbm, gain_ref, load_sem.at[11])]
    for copy in small:
        copy.start()
    x_load.start()

    barrier = pltpu.get_barrier_semaphore()
    greet = list(to.values()) + [sib, z_four[1]] + list(to_y)
    for other in greet:
        pl.semaphore_signal(barrier, inc=1, device_id=other, device_id_type=MESH)
    pl.semaphore_wait(barrier, len(greet))

    def rcopy(src, dst, ssem, rsem, device):
        return pltpu.make_async_remote_copy(src, dst, ssem, rsem, device_id=device, device_id_type=MESH)

    def own_copy(g):
        i0, n, _ = GROUPS[g]
        ref = buf.at[pl.ds(i0, n), x, z, c]
        return rcopy(ref, ref, own_send.at[g], own_recv.at[g], sib)

    for g in range(len(GROUPS)):
        for copy in loads[g]:
            copy.wait()
        own_copy(g).start()

    for copy in small:
        copy.wait()
    pos = lambda shape, dim: lax.broadcasted_iota(jnp.int32, shape, dim).astype(F32)
    log_decay = [jnp.log1p(-(jnp.full((1, HD), codes[h], jnp.int32).astype(F32)) * 1e-06) for h in range(2)]
    ld_mine = jnp.where(c == 0, log_decay[0], log_decay[1])

    def table(r, carry):
        row = pos((64, T), 0) + (r * 64).astype(F32)
        diff = row - pos((64, T), 1)
        for h in range(2):
            ld = jnp.concatenate([log_decay[h]] * (T // HD), axis=1)
            w = jnp.where(diff >= 0, jnp.exp(jnp.maximum(diff, 0.0) * ld), 0.0)
            wts[h, pl.ds(pl.multiple_of(r * 64, 64), 64), :] = w
        return carry

    def piece(g, px, pz, rows, half=None):
        i0, n, _ = GROUPS[g]
        cc = pl.ds(0, 2) if half is None else pl.ds(half, 1)
        return buf.at[pl.ds(i0, n), px, pz, cc, pl.ds(*rows), :]

    def send(g, kind, ref, slot, where):
        rcopy(ref, ref, send_sem.at[g, kind], recv.at[g, slot], to[where]).start()

    def arrived(g, ref, slot):
        rcopy(ref, ref, send_sem.at[g, 0], recv.at[g, slot], sib).wait_recv()

    def relay(g, column, ref):
        rcopy(ref, ref, relay_send.at[g, column], relay_recv.at[g, column], sib).start()

    def event_a(g, slot):
        pc = functools.partial(piece, g, rows=(0, GROUPS[g][2]))
        chain = lambda k, hop, way: 4 + (k * 4 + hop) * 2 + way
        columns = (x, xm, xp, x2)
        if slot < 3:
            k = slot + 1
            ref = pc(columns[k], z)
            if slot >= 0:
                arrived(g, ref, slot)
            else:
                for o, where in enumerate(("xp", "xm", "x2")):
                    send(g, 0, ref, o, where)
            send(g, 1, ref, chain(k, 0, 0), "zp")
            send(g, 1, ref, chain(k, 0, 1), "zm")
            if slot >= 0:
                relay(g, k, ref)
            return
        k, hop, way = (slot - 4) // 8, (slot - 4) // 2 % 4, slot % 2
        pz = (z + (8 - hop - 1 if way == 0 else hop + 1)) % NZ
        ref = pc(columns[k], pz, half=way if hop == 3 else None)
        arrived(g, ref, slot)
        if hop < 3:
            part = pc(columns[k], pz, half=way if hop == 2 else None)
            send(g, 1, part, chain(k, hop + 1, way), ("zp", "zm")[way])
        relay(g, k, ref)

    def event_b(g, slot, last):
        _, _, a = GROUPS[g]
        pc = functools.partial(piece, g, rows=(a, SH - a))
        zs = (0, -1, 1, -2, 2, -3, 3, 4)

        def across(k):
            ref = pc(x, (z + 8 + zs[k]) % NZ)
            send(g, 1, ref, 8 + 4 * k, "xp")
            send(g, 1, ref, 9 + 4 * k, "xm")

        if slot < 0:
            send(g, 0, pc(x, z), 0, "zp")
            send(g, 0, pc(x, z), 1, "zm")
            across(0)
        elif slot < 6:
            ref = pc(x, (z + 8 + zs[slot + 1]) % NZ)
            arrived(g, ref, slot)
            if slot < 4:
                send(g, 0, ref, slot + 2, ("zp", "zm")[slot % 2])
            if slot in (2, 3):
                half = pc(x, (z + 8 + zs[slot + 1]) % NZ, half=slot - 2)
                send(g, 0, half, slot + 4, ("zp2", "zm2")[slot - 2])
            across(slot + 1)
            relay(g, 0, ref)
        elif slot < 8:
            ref = pc(x, z4, half=slot - 6)
            arrived(g, ref, slot)
            relay(g, 0, ref)
            if last:
                across(7)
        else:
            k, j = (slot - 8) // 4, slot % 4
            pz = (z + 8 + zs[k]) % NZ
            ref = pc((xm, xp, x2, x2)[j], pz, half=None if j < 2 else j - 2)
            arrived(g, ref, slot)
            if j < 2:
                send(g, 1, pc((xm, xp)[j], pz, half=j), slot + 2, ("xp", "xm")[j])
            relay(g, (1, 2, 3, 3)[j], ref)

    def events(core, todo, seen):
        for g, slot in todo:
            if slot < 0:
                i0, n, _ = GROUPS[g]
                ref = buf.at[pl.ds(i0, n), x, z, 1 - c]
                rcopy(ref, ref, own_send.at[g], own_recv.at[g], sib).wait_recv()
            if core == 0:
                event_a(g, slot)
            else:
                event_b(g, slot, (g, 13 - slot) in seen)
            seen.add((g, slot))

    def sizes(g, core):
        i0, n, a = GROUPS[g]
        if core == 0:
            return [buf.at[pl.ds(i0, n), pl.ds(0, 3), 0, :, pl.ds(0, a), :],
                    buf.at[pl.ds(i0, n), :, pl.ds(0, 7), :, pl.ds(0, a), :]]
        return [buf.at[pl.ds(i0, n), 0, pl.ds(0, 7), :, pl.ds(a, SH - a), :],
                buf.at[pl.ds(i0, n), pl.ds(0, 3), :, :, pl.ds(a, SH - a), :]]

    def column_size(g, core, column):
        i0, n, a = GROUPS[g]
        rows = pl.ds(0, a) if core == 0 else pl.ds(a, SH - a)
        return buf.at[pl.ds(i0, n), 0, pl.ds(0, 7 if column == 0 else 8), :, rows, :]

    def relays_arrived(g, column):
        for core in range(2):
            @pl.when(c == 1 - core)
            def _(core=core):
                ref = column_size(g, core, column)
                rcopy(ref, ref, relay_send.at[g, 0], relay_recv.at[g, column], sib).wait_recv()

    def sends_done(g):
        own_copy(g).wait_send()
        for core in range(2):
            @pl.when(c == core)
            def _(core=core):
                for kind, ref in enumerate(sizes(g, core)):
                    rcopy(ref, ref, send_sem.at[g, kind], recv.at[g, 0], sib).wait_send()
                for column in range(NX):
                    ref = column_size(g, core, column)
                    rcopy(ref, ref, relay_send.at[g, column], relay_recv.at[g, 0], sib).wait_send()

    def project(item, k):
        px = (x, xm, xp, x2)[k]
        cols = pl.ds(pl.multiple_of(px * KX, KX), KX)
        part = jnp.dot(xv[:, cols], buf[item, px].reshape(KX, F), preferred_element_type=F32)
        if k == 0:
            acc[item] = part
        else:
            acc[item] += part

    def silu(v):
        return v * jax.nn.sigmoid(v)

    def local_state():
        for h in range(2):
            tail = jnp.exp((T - 1.0 - pos((T, HD), 0)) * log_decay[h])
            cols = pl.ds(HD * h, HD)
            kt = (kv[0, :, cols].astype(F32) * tail).astype(BF)
            state[h] = lax.dot_general(kt, kv[1, :, cols], (((0,), (0,)), ((), ())), preferred_element_type=F32)

    whole = lambda n: jnp.exp((n * T) * ld_mine)

    def scan_open():
        rcopy(state.at[1 - c], sx, st_send.at[0, 0], st_recv.at[0, 0], sib).start()

    def scan_chip():
        rcopy(state.at[1 - c], sx, st_send.at[0, 0], st_recv.at[0, 0], sib).wait_recv()
        mine, other = state[c], sx[...]
        first = jnp.where(c == 0, mine, other)
        stg[0] = first
        stg[1] = whole(1.0) * first + jnp.where(c == 0, other, mine)
        stg[2] = jnp.zeros_like(first)

    steps = (((z_pair,), z % 2, 1, 0), (z_four, z // 2, 2, z % 2), (x_four, x, 8, z))

    def scan_send(k):
        snd[k] = stg[1].astype(BF)
        for o, other in enumerate(steps[k][0]):
            rcopy(snd.at[k], rcv.at[k, o], st_send.at[1 + k, o], st_recv.at[1 + k, o], other).start()

    def scan_step(k):
        others, place, span, reach = steps[k]
        count = len(others) + 1
        chips = lambda n: whole(2.0 * jnp.asarray(n, jnp.int32).astype(F32))
        tot = stg[1] * chips((count - 1 - place) * span)
        before = stg[2]
        for o, other in enumerate(others):
            rcopy(snd.at[k], rcv.at[k, o], st_send.at[1 + k, o], st_recv.at[1 + k, o], other).wait_recv()
            got = rcv[k, o].astype(F32)
            source = (place + count - 1 - o) % count
            before += jnp.where(place > o, chips(o * span + reach), 0.0) * got
            tot += chips((count - 1 - source) * span) * got
        stg[1] = tot
        stg[2] = before

    def scan_end():
        low = stg[2]
        high = whole(1.0) * low + stg[0]
        pri[c] = jnp.where(c == 0, low, high)
        stg[3] = jnp.where(c == 0, high, low)
        rcopy(stg.at[3], pri.at[c], st_send.at[0, 1], st_recv.at[0, 1], sib).start()

    def scan_close():
        rcopy(stg.at[3], pri.at[1 - c], st_send.at[0, 1], st_recv.at[0, 1], sib).wait_recv()

    def intra(h, r):
        cols = pl.ds(HD * h, HD)
        rows = pl.ds(128 * r, 128)
        seen = 128 * (r + 1)
        scores = lax.dot_general(qv[rows, cols], kv[0, :seen, cols], (((1,), (1,)), ((), ())), preferred_element_type=F32)
        probs = (scores * wts[h, rows, :seen]).astype(BF)
        att[rows, cols] = jnp.dot(probs, kv[1, :seen, cols], preferred_element_type=F32)

    def inter(h):
        cols = pl.ds(HD * h, HD)
        into = jnp.exp((pos((T, HD), 0) + 1.0) * log_decay[h])
        prior = pri[h]
        top = prior.astype(BF)
        rest = (prior - top.astype(F32)).astype(BF)
        query = qv[:, cols]
        got = jnp.dot(query, top, preferred_element_type=F32) + jnp.dot(query, rest, preferred_element_type=F32)
        full = att[:, cols] + into * got
        scale = lax.rsqrt(jnp.mean(full * full, axis=1, keepdims=True) + 1e-06)
        att[:, cols] = full * scale * gain_ref[:, HD * h:HD * (h + 1)]

    def hcopy(src_y, r, lo, n, slot):
        ref = hid.at[src_y, pl.ds(128 * r + lo, n), :]
        return rcopy(ref, ref, h_send.at[r, slot], h_recv.at[r, slot], to_y[slot % 2])

    def gate(r):
        rows = pl.ds(128 * r, 128)
        hid[y, rows, :] = (att[rows, :] * jax.nn.sigmoid(acc[3, rows, :])).astype(BF)
        hcopy(y, r, 0, 128, 0).start()
        hcopy(y, r, 0, 128, 1).start()

    def forward(r):
        hcopy(ym, r, 0, 128, 0).wait_recv()
        hcopy(ym, r, 0, 64, 2).start()
        hcopy(yp, r, 0, 128, 1).wait_recv()
        hcopy(yp, r, 64, 64, 3).start()

    def far(r):
        hcopy(y2, r, 0, 64, 2).wait_recv()
        hcopy(y2, r, 64, 64, 3).wait_recv()

    def out_part(py, first, last):
        for j in range(6):
            cols = pl.ds(F * j, F)
            w = buf[4, py, :, :, 16 * j:16 * (j + 1), :].reshape(F, F)
            part = jnp.dot(hid[py], w, preferred_element_type=F32)
            if first:
                oacc[:, cols] = part
            elif not last:
                oacc[:, cols] += part
            else:
                outv[:, cols] = (oacc[:, cols] + part).astype(BF)
                pltpu.make_async_copy(outv.at[:, cols], out_hbm.at[:, cols], out_sem.at[j]).start()

    def finish_k():
        kv[0] = silu(acc[0]).astype(BF)

    def finish_v():
        kv[1] = silu(acc[1]).astype(BF)

    def finish_q():
        qv[...] = silu(acc[2]).astype(BF)

    def weights(g, k):
        relays_arrived(g, k)
        if (g, k) == (0, 0):
            x_load.wait()

    def act(name):
        kind, n = name.rstrip("0123"), name[-1]
        n = int(n) if n.isdigit() else None
        if kind == "table":
            lax.fori_loop(0, T // 64, table, 0)
        elif kind in "KVQG":
            item = "KVQG".index(kind)
            if kind != "V":
                weights((0, 0, 1, 2)[item], n)
            project(item, n)
        elif kind == "fin" + name[-1]:
            (finish_k if n is None and name[-1] == "K" else finish_v if name[-1] == "V" else finish_q)()
        elif kind == "state":
            local_state()
            scan_open()
        elif kind == "chip":
            scan_chip()
            scan_send(0)
        elif kind == "st":
            scan_step(n)
            if n < 2:
                scan_send(n + 1)
            else:
                scan_end()
        elif kind == "intra":
            for r in range(4):
                intra(n, r)
        elif kind == "inter":
            scan_close()
            for h in range(2):
                inter(h)
        elif kind == "gate":
            gate(n)
        elif kind == "fwd":
            forward(n)
        elif kind == "out":
            if n == 0:
                for k in range(NX):
                    weights(3, k)
            if n == 3:
                for r in range(4):
                    far(r)
            out_part((y, ym, yp, y2)[n], n == 0, n == 3)

    seen = (set(), set())
    for name, *todo in PLAN:
        for core in range(2):
            if todo[core]:
                @pl.when(c == core)
                def _(core=core, todo=todo):
                    events(core, todo[core], seen[core])
        if name:
            act(name)

    for g in range(len(GROUPS)):
        sends_done(g)
    rcopy(state.at[1 - c], sx, st_send.at[0, 0], st_recv.at[0, 0], sib).wait_send()
    rcopy(stg.at[3], pri.at[c], st_send.at[0, 1], st_recv.at[0, 1], sib).wait_send()
    for k in range(3):
        for o, other in enumerate(steps[k][0]):
            rcopy(snd.at[k], rcv.at[k, o], st_send.at[1 + k, o], st_recv.at[1 + k, o], other).wait_send()
    for r in range(4):
        hcopy(y, r, 0, 128, 0).wait_send()
        hcopy(y, r, 0, 128, 1).wait_send()
        hcopy(ym, r, 0, 64, 2).wait_send()
        hcopy(yp, r, 64, 64, 3).wait_send()
    for j in range(6):
        cols = pl.ds(F * j, F)
        pltpu.make_async_copy(outv.at[:, cols], out_hbm.at[:, cols], out_sem.at[j]).wait()


def shards(inputs, proj_weight, decay_codes, norm_gain, out_weight):
    vmem = pltpu.VMEM
    dma = pltpu.SemaphoreType.DMA
    hbm = pl.BlockSpec(memory_space=pltpu.HBM)
    ng = len(GROUPS)
    args = (inputs, proj_weight, decay_codes, norm_gain.reshape(1, F), out_weight)
    args = [pltpu.with_memory_space_constraint(a, pltpu.HBM) for a in args]
    return pl.pallas_call(
        kernel,
        out_shape=jax.ShapeDtypeStruct((T, 1536), BF),
        in_specs=[hbm] * 5,
        out_specs=pl.BlockSpec(memory_space=pl.ANY),
        scratch_shapes=[
            pltpu.SMEM((2,), jnp.int32),
            vmem((1, F), F32),
            vmem((5, NX, NZ, 2, SH, F), BF),
            vmem((T, D), BF),
            vmem((2, T, T), F32),
            vmem((4, T, F), F32),
            vmem((2, T, F), BF),
            vmem((T, F), BF),
            vmem((T, F), F32),
            vmem((NY, T, F), BF),
            vmem((T, 1536), F32),
            vmem((T, 1536), BF),
            vmem((2, HD, HD), F32),
            vmem((HD, HD), F32),
            vmem((3, HD, HD), BF),
            vmem((3, 3, HD, HD), BF),
            vmem((4, HD, HD), F32),
            vmem((2, HD, HD), F32),
            dma((12,)),
            dma((ng,)),
            dma((ng,)),
            dma((ng, NSLOT)),
            dma((ng, NX)),
            dma((ng, NX)),
            dma((ng, 2)),
            dma((4, 3)),
            dma((4, 3)),
            dma((4, 4)),
            dma((4, 4)),
            dma((6,)),
        ],
        compiler_params=pltpu.CompilerParams(collective_id=0, has_side_effects=True, vmem_limit_bytes=52 * 2 ** 20),
        name="lightning",
    )(*args)


def solution(mesh):
    in_specs = (P("seq", None), P(None, "seq", "tp"), P("tp"), P("tp"), P("seq", "tp"))
    out_specs = P("seq", "tp")
    return jax.shard_map(shards, mesh=mesh, in_specs=in_specs, out_specs=out_specs, check_vma=False)
```

```python
import functools

import jax
import jax.numpy as jnp
from jax import lax
from jax.experimental import pallas as pl
from jax.experimental.pallas import tpu as pltpu
from jax.sharding import PartitionSpec as P

NX, NZ, NY = 4, 8, 4
T = 512
D = 6144
HD = 128
F = 256
SH = 96
KX = D // NX
MESH = pl.DeviceIdType.MESH
BF = jnp.bfloat16
F32 = jnp.float32

NSLOT = 40

GROUPS = ((0, 2, 32), (2, 1, 32), (3, 1, 48), (4, 1, 32))
PLAN = (
    ("table", ((0, -1),),
     ((0, -1),)),
    ("K0", ((0, 0), (0, 1), (0, 4), (0, 5), (0, 2), (0, 12), (0, 13), (0, 20), (0, 21), (0, 6), (0, 7), (1, -1), (0, 28), (0, 29), (0, 14), (0, 15), (1, 0), (1, 1), (0, 22), (0, 23), (1, 2), (0, 8), (0, 9), (1, 4), (1, 5), (0, 30), (0, 31), (2, -1), (0, 16), (0, 17), (1, 12), (1, 13), (1, 20), (1, 21), (0, 24), (0, 25), (1, 28), (1, 29), (2, 0), (2, 1), (0, 10), (0, 11),),
     ((0, 0), (0, 1), (0, 8), (0, 9), (1, -1), (0, 12), (0, 13), (0, 2), (0, 3), (0, 16), (0, 17), (0, 10), (0, 11), (1, 8), (1, 9), (0, 14), (0, 15), (1, 0), (1, 1), (2, -1), (0, 20), (0, 21), (0, 4), (0, 5), (0, 24), (0, 25), (0, 18), (0, 19), (1, 10), (1, 11), (0, 6), (0, 7), (1, 12), (1, 13), (1, 16), (1, 17), (2, 8), (2, 9), (0, 22), (0, 23), (1, 2), (1, 3),)),
    ("V0", ((1, 6), (1, 7), (2, 2),),
     ()),
    ("K1", ((0, 32), (0, 33), (2, 4), (2, 5), (0, 18), (0, 19), (1, 14), (1, 15), (1, 22), (1, 23), (0, 26), (0, 27), (1, 30), (1, 31), (2, 12), (2, 13), (2, 20), (2, 21), (1, 8), (1, 9), (2, 28), (2, 29),),
     ((2, 0), (2, 1), (0, 28), (0, 29), (0, 32), (0, 33), (0, 26), (0, 27), (0, 36), (0, 37),)),
    ("K2", (),
     ((1, 14), (1, 15), (1, 18), (1, 19), (2, 10), (2, 11),)),
    ("V1", ((0, 34), (0, 35),),
     ((1, 4), (1, 5), (1, 20), (1, 21),)),
    ("V2", ((3, -1),),
     ((1, 24), (1, 25), (1, 6), (3, -1), (1, 7), (2, 2), (2, 3), (2, 12), (2, 13), (2, 16), (2, 17),)),
    ("Q0", ((2, 6), (2, 7), (1, 16), (1, 17), (1, 24), (1, 25), (1, 32), (1, 33), (2, 14), (2, 15), (2, 22), (2, 23), (1, 10), (1, 11),),
     ((0, 30), (0, 31), (0, 34), (0, 35), (0, 38), (0, 39), (1, 28), (1, 29), (3, 0), (3, 1), (1, 32), (1, 33), (1, 22), (1, 23),)),
    ("K3", ((2, 30), (2, 31),),
     ((1, 26), (1, 27), (2, 4), (2, 5), (3, 8), (3, 9),)),
    ("V3", ((3, 4), (3, 5),),
     ((2, 6), (2, 7), (1, 36), (1, 37),)),
    ("finK", (),
     ()),
    ("finV", (),
     ()),
    ("state", (),
     ()),
    ("chip", ((2, 8), (2, 9), (1, 18), (1, 19), (1, 26), (1, 27), (1, 34), (1, 35), (3, 0), (3, 1), (2, 16), (2, 17), (3, 2), (2, 24), (2, 25), (2, 32), (2, 33),),
     ((2, 20), (2, 21), (2, 24), (2, 25),)),
    ("Q1", ((3, 6), (3, 7),),
     ((2, 14), (2, 15), (2, 18), (2, 19),)),
    ("Q2", ((2, 10), (2, 11), (3, 12), (3, 13), (3, 20), (3, 21), (2, 18), (2, 19),),
     ((3, 2), (3, 3), (1, 30), (1, 31), (3, 12), (3, 13),)),
    ("G0", ((3, 28), (3, 29), (2, 26), (2, 27), (2, 34), (2, 35),),
     ((3, 16), (3, 17), (1, 34), (1, 35), (2, 28), (2, 29),)),
    ("st0", (),
     ((2, 32), (2, 33),)),
    ("G1", ((3, 8), (3, 9), (3, 14), (3, 15),),
     ((3, 10), (3, 11), (3, 4), (3, 5), (2, 36), (2, 37),)),
    ("G2", ((3, 22), (3, 23), (3, 30), (3, 31),),
     ((1, 38), (1, 39), (2, 22), (2, 23), (2, 26), (2, 27), (3, 6), (3, 7),)),
    ("Q3", (),
     ((3, 20), (3, 21),)),
    ("finQ", (),
     ((3, 24), (3, 25), (3, 14), (3, 15),)),
    ("intra0", (),
     ((3, 18), (3, 19),)),
    ("st1", ((3, 10), (3, 11),),
     ((2, 30), (2, 31), (2, 34), (2, 35),)),
    ("intra1", ((3, 16), (3, 17), (3, 24), (3, 25),),
     ()),
    ("G3", ((3, 32), (3, 33),),
     ((3, 28), (3, 29), (3, 32), (3, 33), (2, 38), (2, 39),)),
    ("st2", ((3, 18), (3, 19), (3, 26), (3, 27), (3, 34), (3, 35),),
     ((3, 36), (3, 37), (3, 22), (3, 23), (3, 26), (3, 27), (3, 30), (3, 31),)),
    ("inter", (),
     ((3, 34), (3, 35), (3, 38), (3, 39),)),
    ("gate0", (),
     ()),
    ("gate1", (),
     ()),
    ("gate2", (),
     ()),
    ("gate3", (),
     ()),
    ("out0", (),
     ()),
    ("fwd0", (),
     ()),
    ("fwd1", (),
     ()),
    ("fwd2", (),
     ()),
    ("fwd3", (),
     ()),
    ("out1", (),
     ()),
    ("out2", (),
     ()),
    ("out3", (),
     ()),
)


def kernel(x_hbm, wp_hbm, codes_hbm, gain_hbm, wo_hbm, out_ref,
           codes, gain_ref, buf, xv, wts, acc, kv, qv, att, hid, oacc,
           state, sx, snd, rcv, stg, pri,
           load_sem, own_send, own_recv, recv, relay_recv, relay_send, send_sem,
           st_send, st_recv, h_send, h_recv):
    s = lax.axis_index("seq")
    y = lax.axis_index("tp")
    x, z, c = s // 16, (s // 2) % 8, s % 2
    q = s // 2

    def dev(px, pz, pc, py):
        return {"seq": (px * NZ + pz) * 2 + pc, "tp": py}

    xp, xm = (x + 1) % NX, (x + 3) % NX
    zp, zm = (z + 1) % NZ, (z + 7) % NZ
    yp, ym = (y + 1) % NY, (y + 3) % NY
    x2, z4, y2 = (x + 2) % NX, (z + 4) % NZ, (y + 2) % NY
    sib = dev(x, z, 1 - c, y)
    zp2, zm2 = (z + 2) % NZ, (z + 6) % NZ
    to = {"xp": dev(xp, z, c, y), "xm": dev(xm, z, c, y), "zp": dev(x, zp, c, y), "zm": dev(x, zm, c, y),
          "x2": dev(x2, z, c, y), "zp2": dev(x, zp2, c, y), "zm2": dev(x, zm2, c, y)}
    to_y = (dev(x, z, c, yp), dev(x, z, c, ym))
    z_pair = dev(x, z + 1 - 2 * (z % 2), c, y)
    z_four = (to["zp2"], dev(x, z4, c, y), to["zm2"])
    x_four = (to["xp"], to["x2"], to["xm"])

    x_load = pltpu.make_async_copy(x_hbm, xv, load_sem.at[0])
    loads = [
        [pltpu.make_async_copy(wp_hbm.at[pl.ds(1, 2)], buf.at[pl.ds(0, 2), x, z, c], load_sem.at[1])],
        [pltpu.make_async_copy(wp_hbm.at[pl.ds(0, 1)], buf.at[pl.ds(2, 1), x, z, c], load_sem.at[2])],
        [pltpu.make_async_copy(wp_hbm.at[pl.ds(3, 1)], buf.at[pl.ds(3, 1), x, z, c], load_sem.at[3])],
        [pltpu.make_async_copy(wo_hbm.at[:, pl.ds(F * j, F)], buf.at[4, x, z, c, pl.ds(16 * j, 16), :], load_sem.at[4 + j])
         for j in range(6)],
    ]
    for group in loads:
        for copy in group:
            copy.start()
    small = [pltpu.make_async_copy(codes_hbm, codes, load_sem.at[10]),
             pltpu.make_async_copy(gain_hbm, gain_ref, load_sem.at[11])]
    for copy in small:
        copy.start()
    x_load.start()

    barrier = pltpu.get_barrier_semaphore()
    greet = list(to.values()) + [sib, z_four[1]] + list(to_y)
    for other in greet:
        pl.semaphore_signal(barrier, inc=1, device_id=other, device_id_type=MESH)
    pl.semaphore_wait(barrier, len(greet))

    def rcopy(src, dst, ssem, rsem, device):
        return pltpu.make_async_remote_copy(src, dst, ssem, rsem, device_id=device, device_id_type=MESH)

    def own_copy(g):
        i0, n, _ = GROUPS[g]
        ref = buf.at[pl.ds(i0, n), x, z, c]
        return rcopy(ref, ref, own_send.at[g], own_recv.at[g], sib)

    for g in range(len(GROUPS)):
        for copy in loads[g]:
            copy.wait()
        own_copy(g).start()

    for copy in small:
        copy.wait()
    pos = lambda shape, dim: lax.broadcasted_iota(jnp.int32, shape, dim).astype(F32)
    log_decay = [jnp.log1p(-(jnp.full((1, HD), codes[h], jnp.int32).astype(F32)) * 1e-06) for h in range(2)]
    ld_mine = jnp.where(c == 0, log_decay[0], log_decay[1])

    def table(r, carry):
        row = pos((64, T), 0) + (r * 64).astype(F32)
        diff = row - pos((64, T), 1)
        for h in range(2):
            ld = jnp.concatenate([log_decay[h]] * (T // HD), axis=1)
            w = jnp.where(diff >= 0, jnp.exp(jnp.maximum(diff, 0.0) * ld), 0.0)
            wts[h, pl.ds(pl.multiple_of(r * 64, 64), 64), :] = w
        return carry

    def piece(g, px, pz, rows, half=None):
        i0, n, _ = GROUPS[g]
        cc = pl.ds(0, 2) if half is None else pl.ds(half, 1)
        return buf.at[pl.ds(i0, n), px, pz, cc, pl.ds(*rows), :]

    def send(g, kind, ref, slot, where):
        rcopy(ref, ref, send_sem.at[g, kind], recv.at[g, slot], to[where]).start()

    def arrived(g, ref, slot):
        rcopy(ref, ref, send_sem.at[g, 0], recv.at[g, slot], sib).wait_recv()

    def relay(g, column, ref):
        rcopy(ref, ref, relay_send.at[g, column], relay_recv.at[g, column], sib).start()

    def own_arrived(g):
        i0, n, _ = GROUPS[g]
        ref = buf.at[pl.ds(i0, n), x, z, 1 - c]
        rcopy(ref, ref, own_send.at[g], own_recv.at[g], sib).wait_recv()

    def event_a(g, slot):
        pc = functools.partial(piece, g, rows=(0, GROUPS[g][2]))
        chain = lambda k, hop, way: 4 + (k * 4 + hop) * 2 + way
        columns = (x, xm, xp, x2)
        if slot < 3:
            k = slot + 1
            if slot >= 0:
                arrived(g, pc(columns[k], z), slot)
            for half in ((0, 1) if (g, slot) == (0, -1) else (None,)):
                ref = pc(columns[k], z, half=half)
                if slot < 0:
                    if half != 0:
                        own_arrived(g)
                    for o, where in enumerate(("xp", "xm", "x2")):
                        send(g, 0, ref, o, where)
                send(g, 1, ref, chain(k, 0, 0), "zp")
                send(g, 1, ref, chain(k, 0, 1), "zm")
            if slot >= 0:
                relay(g, k, ref)
            return
        k, hop, way = (slot - 4) // 8, (slot - 4) // 2 % 4, slot % 2
        pz = (z + (8 - hop - 1 if way == 0 else hop + 1)) % NZ
        ref = pc(columns[k], pz, half=way if hop == 3 else None)
        arrived(g, ref, slot)
        if hop < 3:
            part = pc(columns[k], pz, half=way if hop == 2 else None)
            send(g, 1, part, chain(k, hop + 1, way), ("zp", "zm")[way])
        relay(g, k, ref)

    def event_b(g, slot, last):
        _, _, a = GROUPS[g]
        pc = functools.partial(piece, g, rows=(a, SH - a))
        zs = (0, -1, 1, -2, 2, -3, 3, 4)

        def across(k):
            ref = pc(x, (z + 8 + zs[k]) % NZ)
            send(g, 1, ref, 8 + 4 * k, "xp")
            send(g, 1, ref, 9 + 4 * k, "xm")

        if slot < 0:
            for half in ((1, 0) if g == 0 else (None,)):
                if half != 1:
                    own_arrived(g)
                ref = pc(x, z, half=half)
                send(g, 0, ref, 0, "zp")
                send(g, 0, ref, 1, "zm")
                send(g, 1, ref, 8, "xp")
                send(g, 1, ref, 9, "xm")
        elif slot < 6:
            ref = pc(x, (z + 8 + zs[slot + 1]) % NZ)
            arrived(g, ref, slot)
            if slot < 4:
                send(g, 0, ref, slot + 2, ("zp", "zm")[slot % 2])
            if slot in (2, 3):
                half = pc(x, (z + 8 + zs[slot + 1]) % NZ, half=slot - 2)
                send(g, 0, half, slot + 4, ("zp2", "zm2")[slot - 2])
            across(slot + 1)
            relay(g, 0, ref)
        elif slot < 8:
            ref = pc(x, z4, half=slot - 6)
            arrived(g, ref, slot)
            relay(g, 0, ref)
            if last:
                across(7)
        else:
            k, j = (slot - 8) // 4, slot % 4
            pz = (z + 8 + zs[k]) % NZ
            ref = pc((xm, xp, x2, x2)[j], pz, half=None if j < 2 else j - 2)
            arrived(g, ref, slot)
            if j < 2:
                send(g, 1, pc((xm, xp)[j], pz, half=j), slot + 2, ("xp", "xm")[j])
            relay(g, (1, 2, 3, 3)[j], ref)

    def events(core, todo, seen):
        for g, slot in todo:
            if core == 0:
                event_a(g, slot)
            else:
                event_b(g, slot, (g, 13 - slot) in seen)
            seen.add((g, slot))

    def sizes(g, core):
        i0, n, a = GROUPS[g]
        if core == 0:
            return [buf.at[pl.ds(i0, n), pl.ds(0, 3), 0, :, pl.ds(0, a), :],
                    buf.at[pl.ds(i0, n), :, pl.ds(0, 7), :, pl.ds(0, a), :]]
        return [buf.at[pl.ds(i0, n), 0, pl.ds(0, 7), :, pl.ds(a, SH - a), :],
                buf.at[pl.ds(i0, n), pl.ds(0, 3), :, :, pl.ds(a, SH - a), :]]

    def column_size(g, core, column):
        i0, n, a = GROUPS[g]
        rows = pl.ds(0, a) if core == 0 else pl.ds(a, SH - a)
        return buf.at[pl.ds(i0, n), 0, pl.ds(0, 7 if column == 0 else 8), :, rows, :]

    def relays_arrived(g, column):
        for core in range(2):
            @pl.when(c == 1 - core)
            def _(core=core):
                ref = column_size(g, core, column)
                rcopy(ref, ref, relay_send.at[g, 0], relay_recv.at[g, column], sib).wait_recv()

    def sends_done(g):
        own_copy(g).wait_send()
        for core in range(2):
            @pl.when(c == core)
            def _(core=core):
                for kind, ref in enumerate(sizes(g, core)):
                    rcopy(ref, ref, send_sem.at[g, kind], recv.at[g, 0], sib).wait_send()
                for column in range(NX):
                    ref = column_size(g, core, column)
                    rcopy(ref, ref, relay_send.at[g, column], relay_recv.at[g, 0], sib).wait_send()

    def project(item, k):
        px = (x, xm, xp, x2)[k]
        cols = pl.ds(pl.multiple_of(px * KX, KX), KX)
        part = jnp.dot(xv[:, cols], buf[item, px].reshape(KX, F), preferred_element_type=F32)
        if k == 0:
            acc[item] = part
        else:
            acc[item] += part

    def silu(v):
        return v * jax.nn.sigmoid(v)

    def local_state():
        for h in range(2):
            tail = jnp.exp((T - 1.0 - pos((T, HD), 0)) * log_decay[h])
            cols = pl.ds(HD * h, HD)
            kt = (kv[0, :, cols].astype(F32) * tail).astype(BF)
            state[h] = lax.dot_general(kt, kv[1, :, cols], (((0,), (0,)), ((), ())), preferred_element_type=F32)

    whole = lambda n: jnp.exp((n * T) * ld_mine)

    def scan_open():
        rcopy(state.at[1 - c], sx, st_send.at[0, 0], st_recv.at[0, 0], sib).start()

    def scan_chip():
        rcopy(state.at[1 - c], sx, st_send.at[0, 0], st_recv.at[0, 0], sib).wait_recv()
        mine, other = state[c], sx[...]
        first = jnp.where(c == 0, mine, other)
        stg[0] = first
        stg[1] = whole(1.0) * first + jnp.where(c == 0, other, mine)
        stg[2] = jnp.zeros_like(first)

    steps = (((z_pair,), z % 2, 1, 0), (z_four, z // 2, 2, z % 2), (x_four, x, 8, z))

    def scan_send(k):
        snd[k] = stg[1].astype(BF)
        for o, other in enumerate(steps[k][0]):
            rcopy(snd.at[k], rcv.at[k, o], st_send.at[1 + k, o], st_recv.at[1 + k, o], other).start()

    def scan_step(k):
        others, place, span, reach = steps[k]
        count = len(others) + 1
        chips = lambda n: whole(2.0 * jnp.asarray(n, jnp.int32).astype(F32))
        tot = stg[1] * chips((count - 1 - place) * span)
        before = stg[2]
        for o, other in enumerate(others):
            rcopy(snd.at[k], rcv.at[k, o], st_send.at[1 + k, o], st_recv.at[1 + k, o], other).wait_recv()
            got = rcv[k, o].astype(F32)
            source = (place + count - 1 - o) % count
            before += jnp.where(place > o, chips(o * span + reach), 0.0) * got
            tot += chips((count - 1 - source) * span) * got
        stg[1] = tot
        stg[2] = before

    def scan_end():
        low = stg[2]
        high = whole(1.0) * low + stg[0]
        pri[c] = jnp.where(c == 0, low, high)
        stg[3] = jnp.where(c == 0, high, low)
        rcopy(stg.at[3], pri.at[c], st_send.at[0, 1], st_recv.at[0, 1], sib).start()

    def scan_close():
        rcopy(stg.at[3], pri.at[1 - c], st_send.at[0, 1], st_recv.at[0, 1], sib).wait_recv()

    def intra(h, r):
        cols = pl.ds(HD * h, HD)
        rows = pl.ds(128 * r, 128)
        seen = 128 * (r + 1)
        scores = lax.dot_general(qv[rows, cols], kv[0, :seen, cols], (((1,), (1,)), ((), ())), preferred_element_type=F32)
        probs = (scores * wts[h, rows, :seen]).astype(BF)
        att[rows, cols] = jnp.dot(probs, kv[1, :seen, cols], preferred_element_type=F32)

    def inter(h):
        cols = pl.ds(HD * h, HD)
        into = jnp.exp((pos((T, HD), 0) + 1.0) * log_decay[h])
        prior = pri[h]
        top = prior.astype(BF)
        rest = (prior - top.astype(F32)).astype(BF)
        query = qv[:, cols]
        got = jnp.dot(query, top, preferred_element_type=F32) + jnp.dot(query, rest, preferred_element_type=F32)
        full = att[:, cols] + into * got
        scale = lax.rsqrt(jnp.mean(full * full, axis=1, keepdims=True) + 1e-06)
        att[:, cols] = full * scale * gain_ref[:, HD * h:HD * (h + 1)]

    def hcopy(src_y, r, lo, n, slot):
        ref = hid.at[src_y, pl.ds(128 * r + lo, n), :]
        return rcopy(ref, ref, h_send.at[r, slot], h_recv.at[r, slot], to_y[slot % 2])

    def gate(r):
        rows = pl.ds(128 * r, 128)
        hid[y, rows, :] = (att[rows, :] * jax.nn.sigmoid(acc[3, rows, :])).astype(BF)
        hcopy(y, r, 0, 128, 0).start()
        hcopy(y, r, 0, 128, 1).start()

    def forward(r):
        hcopy(ym, r, 0, 128, 0).wait_recv()
        hcopy(ym, r, 0, 64, 2).start()
        hcopy(yp, r, 0, 128, 1).wait_recv()
        hcopy(yp, r, 64, 64, 3).start()

    def far(r):
        hcopy(y2, r, 0, 64, 2).wait_recv()
        hcopy(y2, r, 64, 64, 3).wait_recv()

    def out_part(py, first):
        for j in range(6):
            cols = pl.ds(F * j, F)
            w = buf[4, py, :, :, 16 * j:16 * (j + 1), :].reshape(F, F)
            part = jnp.dot(hid[py], w, preferred_element_type=F32)
            if first:
                oacc[:, cols] = part
            else:
                oacc[:, cols] += part

    def out_last(lo, n):
        rows = pl.ds(lo, n)
        for j in range(6):
            cols = pl.ds(F * j, F)
            w = buf[4, y2, :, :, 16 * j:16 * (j + 1), :].reshape(F, F)
            part = jnp.dot(hid[y2, rows, :], w, preferred_element_type=F32)
            out_ref[rows, cols] = (oacc[rows, cols] + part).astype(BF)

    def finish_k():
        kv[0] = silu(acc[0]).astype(BF)

    def finish_v():
        kv[1] = silu(acc[1]).astype(BF)

    def finish_q():
        qv[...] = silu(acc[2]).astype(BF)

    def weights(g, k):
        relays_arrived(g, k)
        if (g, k) == (0, 0):
            x_load.wait()

    def act(name):
        kind, n = name.rstrip("0123"), name[-1]
        n = int(n) if n.isdigit() else None
        if kind == "table":
            lax.fori_loop(0, T // 64, table, 0)
        elif kind in "KVQG":
            item = "KVQG".index(kind)
            if kind != "V":
                weights((0, 0, 1, 2)[item], n)
            project(item, n)
        elif kind == "fin" + name[-1]:
            (finish_k if n is None and name[-1] == "K" else finish_v if name[-1] == "V" else finish_q)()
        elif kind == "state":
            local_state()
            scan_open()
        elif kind == "chip":
            scan_chip()
            scan_send(0)
        elif kind == "st":
            scan_step(n)
            if n < 2:
                scan_send(n + 1)
            else:
                scan_end()
        elif kind == "intra":
            for r in range(4):
                intra(n, r)
        elif kind == "inter":
            scan_close()
            for h in range(2):
                inter(h)
        elif kind == "gate":
            gate(n)
        elif kind == "fwd":
            forward(n)
        elif kind == "out":
            if n == 0:
                for k in range(NX):
                    weights(3, k)
            if n < 3:
                out_part((y, ym, yp)[n], n == 0)
            else:
                for half in range(2):
                    far(2 * half)
                    far(2 * half + 1)
                    out_last(256 * half, 256)

    seen = (set(), set())
    for name, *todo in PLAN:
        for core in range(2):
            if todo[core]:
                @pl.when(c == core)
                def _(core=core, todo=todo):
                    events(core, todo[core], seen[core])
        if name:
            act(name)

    for g in range(len(GROUPS)):
        sends_done(g)
    rcopy(state.at[1 - c], sx, st_send.at[0, 0], st_recv.at[0, 0], sib).wait_send()
    rcopy(stg.at[3], pri.at[c], st_send.at[0, 1], st_recv.at[0, 1], sib).wait_send()
    for k in range(3):
        for o, other in enumerate(steps[k][0]):
            rcopy(snd.at[k], rcv.at[k, o], st_send.at[1 + k, o], st_recv.at[1 + k, o], other).wait_send()
    for r in range(4):
        hcopy(y, r, 0, 128, 0).wait_send()
        hcopy(y, r, 0, 128, 1).wait_send()
        hcopy(ym, r, 0, 64, 2).wait_send()
        hcopy(yp, r, 64, 64, 3).wait_send()

def shards(inputs, proj_weight, decay_codes, norm_gain, out_weight):
    vmem = pltpu.VMEM
    dma = pltpu.SemaphoreType.DMA
    hbm = pl.BlockSpec(memory_space=pltpu.HBM)
    ng = len(GROUPS)
    args = (inputs, proj_weight, decay_codes, norm_gain.reshape(1, F), out_weight)
    args = [pltpu.with_memory_space_constraint(a, pltpu.HBM) for a in args]
    return pl.pallas_call(
        kernel,
        out_shape=jax.ShapeDtypeStruct((T, 1536), BF),
        in_specs=[hbm] * 5,
        out_specs=pl.BlockSpec(memory_space=vmem),
        scratch_shapes=[
            pltpu.SMEM((2,), jnp.int32),
            vmem((1, F), F32),
            vmem((5, NX, NZ, 2, SH, F), BF),
            vmem((T, D), BF),
            vmem((2, T, T), F32),
            vmem((4, T, F), F32),
            vmem((2, T, F), BF),
            vmem((T, F), BF),
            vmem((T, F), F32),
            vmem((NY, T, F), BF),
            vmem((T, 1536), F32),
            vmem((2, HD, HD), F32),
            vmem((HD, HD), F32),
            vmem((3, HD, HD), BF),
            vmem((3, 3, HD, HD), BF),
            vmem((4, HD, HD), F32),
            vmem((2, HD, HD), F32),
            dma((12,)),
            dma((ng,)),
            dma((ng,)),
            dma((ng, NSLOT)),
            dma((ng, NX)),
            dma((ng, NX)),
            dma((ng, 2)),
            dma((4, 3)),
            dma((4, 3)),
            dma((4, 4)),
            dma((4, 4)),
        ],
        compiler_params=pltpu.CompilerParams(collective_id=0, has_side_effects=True, vmem_limit_bytes=52 * 2 ** 20),
        name="lightning",
    )(*args)


def solution(mesh):
    in_specs = (P("seq", None), P(None, "seq", "tp"), P("tp"), P("tp"), P("seq", "tp"))
    out_specs = P("seq", "tp")
    return jax.shard_map(shards, mesh=mesh, in_specs=in_specs, out_specs=out_specs, check_vma=False)
```

```python
import functools

import jax
import jax.numpy as jnp
from jax import lax
from jax.experimental import pallas as pl
from jax.experimental.pallas import tpu as pltpu
from jax.sharding import PartitionSpec as P

NX, NZ, NY = 4, 8, 4
T = 512
D = 6144
HD = 128
F = 256
SH = 96
KX = D // NX
MESH = pl.DeviceIdType.MESH
BF = jnp.bfloat16
F32 = jnp.float32

NSLOT = 40

GROUPS = ((0, 2, 32), (2, 1, 32), (3, 1, 48), (4, 1, 32))
PLAN = (
    ("table", ((0, -1),),
     ((0, -1),)),
    ("K0", ((0, 0), (0, 1), (0, 4), (0, 5), (0, 2), (0, 12), (0, 13), (0, 20), (0, 21), (0, 6), (0, 7), (1, -1), (0, 28), (0, 29), (0, 14), (0, 15), (1, 0), (1, 1), (0, 22), (0, 23), (1, 2), (0, 8), (0, 9), (1, 4), (1, 5), (0, 30), (0, 31), (2, -1), (0, 16), (0, 17), (1, 12), (1, 13), (1, 20), (1, 21), (0, 24), (0, 25), (1, 28), (1, 29), (2, 0), (2, 1), (0, 10), (0, 11),),
     ((0, 0), (0, 1), (0, 8), (0, 9), (1, -1), (0, 12), (0, 13), (0, 2), (0, 3), (0, 16), (0, 17), (0, 10), (0, 11), (1, 8), (1, 9), (0, 14), (0, 15), (1, 0), (1, 1), (2, -1), (0, 20), (0, 21), (0, 4), (0, 5), (0, 24), (0, 25), (0, 18), (0, 19), (1, 10), (1, 11), (0, 6), (0, 7), (1, 12), (1, 13), (1, 16), (1, 17), (2, 8), (2, 9), (0, 22), (0, 23), (1, 2), (1, 3),)),
    ("V0", ((1, 6), (1, 7), (2, 2),),
     ()),
    ("K1", ((0, 32), (0, 33), (2, 4), (2, 5), (0, 18), (0, 19), (1, 14), (1, 15), (1, 22), (1, 23), (0, 26), (0, 27), (1, 30), (1, 31), (2, 12), (2, 13), (2, 20), (2, 21), (1, 8), (1, 9), (2, 28), (2, 29),),
     ((2, 0), (2, 1), (0, 28), (0, 29), (0, 32), (0, 33), (0, 26), (0, 27), (0, 36), (0, 37),)),
    ("K2", (),
     ((1, 14), (1, 15), (1, 18), (1, 19), (2, 10), (2, 11),)),
    ("V1", ((0, 34), (0, 35),),
     ((1, 4), (1, 5), (1, 20), (1, 21),)),
    ("V2", ((3, -1),),
     ((1, 24), (1, 25), (1, 6), (3, -1), (1, 7), (2, 2), (2, 3), (2, 12), (2, 13), (2, 16), (2, 17),)),
    ("Q0", ((2, 6), (2, 7), (1, 16), (1, 17), (1, 24), (1, 25), (1, 32), (1, 33), (2, 14), (2, 15), (2, 22), (2, 23), (1, 10), (1, 11),),
     ((0, 30), (0, 31), (0, 34), (0, 35), (0, 38), (0, 39), (1, 28), (1, 29), (3, 0), (3, 1), (1, 32), (1, 33), (1, 22), (1, 23),)),
    ("K3", ((2, 30), (2, 31),),
     ((1, 26), (1, 27), (2, 4), (2, 5), (3, 8), (3, 9),)),
    ("V3", ((3, 4), (3, 5),),
     ((2, 6), (2, 7), (1, 36), (1, 37),)),
    ("finK", (),
     ()),
    ("finV", (),
     ()),
    ("state", (),
     ()),
    ("chip", ((2, 8), (2, 9), (1, 18), (1, 19), (1, 26), (1, 27), (1, 34), (1, 35), (3, 0), (3, 1), (2, 16), (2, 17), (3, 2), (2, 24), (2, 25), (2, 32), (2, 33),),
     ((2, 20), (2, 21), (2, 24), (2, 25),)),
    ("Q1", ((3, 6), (3, 7),),
     ((2, 14), (2, 15), (2, 18), (2, 19),)),
    ("Q2", ((2, 10), (2, 11), (3, 12), (3, 13), (3, 20), (3, 21), (2, 18), (2, 19),),
     ((3, 2), (3, 3), (1, 30), (1, 31), (3, 12), (3, 13),)),
    ("G0", ((3, 28), (3, 29), (2, 26), (2, 27), (2, 34), (2, 35),),
     ((3, 16), (3, 17), (1, 34), (1, 35), (2, 28), (2, 29),)),
    ("st0", (),
     ((2, 32), (2, 33),)),
    ("G1", ((3, 8), (3, 9), (3, 14), (3, 15),),
     ((3, 10), (3, 11), (3, 4), (3, 5), (2, 36), (2, 37),)),
    ("G2", ((3, 22), (3, 23), (3, 30), (3, 31),),
     ((1, 38), (1, 39), (2, 22), (2, 23), (2, 26), (2, 27), (3, 6), (3, 7),)),
    ("Q3", (),
     ((3, 20), (3, 21),)),
    ("finQ", (),
     ((3, 24), (3, 25), (3, 14), (3, 15),)),
    ("intra0", (),
     ((3, 18), (3, 19),)),
    ("st1", ((3, 10), (3, 11),),
     ((2, 30), (2, 31), (2, 34), (2, 35),)),
    ("intra1", ((3, 16), (3, 17), (3, 24), (3, 25),),
     ()),
    ("G3", ((3, 32), (3, 33),),
     ((3, 28), (3, 29), (3, 32), (3, 33), (2, 38), (2, 39),)),
    ("st2", ((3, 18), (3, 19), (3, 26), (3, 27), (3, 34), (3, 35),),
     ((3, 36), (3, 37), (3, 22), (3, 23), (3, 26), (3, 27), (3, 30), (3, 31),)),
    ("inter", (),
     ((3, 34), (3, 35), (3, 38), (3, 39),)),
    ("gate0", (),
     ()),
    ("gate1", (),
     ()),
    ("gate2", (),
     ()),
    ("gate3", (),
     ()),
    ("out0", (),
     ()),
    ("fwd0", (),
     ()),
    ("fwd1", (),
     ()),
    ("fwd2", (),
     ()),
    ("fwd3", (),
     ()),
    ("out1", (),
     ()),
    ("out2", (),
     ()),
    ("out3", (),
     ()),
)


def kernel(x_hbm, wp_hbm, codes_hbm, gain_hbm, wo_hbm, out_ref,
           codes, gain_ref, buf, xv, wts, acc, kv, qv, att, hid, oacc,
           state, sx, snd, rcv, stg, pri,
           load_sem, own_send, own_recv, recv, relay_recv, relay_send, send_sem,
           st_send, st_recv, h_send, h_recv):
    s = lax.axis_index("seq")
    y = lax.axis_index("tp")
    x, z, c = s // 16, (s // 2) % 8, s % 2
    q = s // 2

    def dev(px, pz, pc, py):
        return {"seq": (px * NZ + pz) * 2 + pc, "tp": py}

    xp, xm = (x + 1) % NX, (x + 3) % NX
    zp, zm = (z + 1) % NZ, (z + 7) % NZ
    yp, ym = (y + 1) % NY, (y + 3) % NY
    x2, z4, y2 = (x + 2) % NX, (z + 4) % NZ, (y + 2) % NY
    sib = dev(x, z, 1 - c, y)
    zp2, zm2 = (z + 2) % NZ, (z + 6) % NZ
    to = {"xp": dev(xp, z, c, y), "xm": dev(xm, z, c, y), "zp": dev(x, zp, c, y), "zm": dev(x, zm, c, y),
          "x2": dev(x2, z, c, y), "zp2": dev(x, zp2, c, y), "zm2": dev(x, zm2, c, y)}
    to_y = (dev(x, z, c, yp), dev(x, z, c, ym))
    z_pair = dev(x, z + 1 - 2 * (z % 2), c, y)
    z_four = (to["zp2"], dev(x, z4, c, y), to["zm2"])
    x_four = (to["xp"], to["x2"], to["xm"])

    x_load = pltpu.make_async_copy(x_hbm, xv, load_sem.at[0])
    loads = [
        [pltpu.make_async_copy(wp_hbm.at[pl.ds(1, 2)], buf.at[pl.ds(0, 2), x, z, c], load_sem.at[1])],
        [pltpu.make_async_copy(wp_hbm.at[pl.ds(0, 1)], buf.at[pl.ds(2, 1), x, z, c], load_sem.at[2])],
        [pltpu.make_async_copy(wp_hbm.at[pl.ds(3, 1)], buf.at[pl.ds(3, 1), x, z, c], load_sem.at[3])],
        [pltpu.make_async_copy(wo_hbm.at[:, pl.ds(F * j, F)], buf.at[4, x, z, c, pl.ds(16 * j, 16), :], load_sem.at[4 + j])
         for j in range(6)],
    ]
    for group in loads:
        for copy in group:
            copy.start()
    small = [pltpu.make_async_copy(codes_hbm, codes, load_sem.at[10]),
             pltpu.make_async_copy(gain_hbm, gain_ref, load_sem.at[11])]
    for copy in small:
        copy.start()
    x_load.start()

    barrier = pltpu.get_barrier_semaphore()
    greet = list(to.values()) + [sib, z_four[1]] + list(to_y)
    for other in greet:
        pl.semaphore_signal(barrier, inc=1, device_id=other, device_id_type=MESH)
    pl.semaphore_wait(barrier, len(greet))

    def rcopy(src, dst, ssem, rsem, device):
        return pltpu.make_async_remote_copy(src, dst, ssem, rsem, device_id=device, device_id_type=MESH)

    def own_copy(g):
        i0, n, _ = GROUPS[g]
        ref = buf.at[pl.ds(i0, n), x, z, c]
        return rcopy(ref, ref, own_send.at[g], own_recv.at[g], sib)

    def share(g):
        for copy in loads[g]:
            copy.wait()
        own_copy(g).start()

    share(0)

    pos = lambda shape, dim: lax.broadcasted_iota(jnp.int32, shape, dim).astype(F32)
    log_decay = []

    def read_decays():
        for copy in small:
            copy.wait()
        log_decay.extend([jnp.log1p(-(jnp.full((1, HD), codes[h], jnp.int32).astype(F32)) * 1e-06) for h in range(2)])

    def table(r, carry):
        row = pos((64, T), 0) + (r * 64).astype(F32)
        diff = row - pos((64, T), 1)
        for h in range(2):
            ld = jnp.concatenate([log_decay[h]] * (T // HD), axis=1)
            w = jnp.where(diff >= 0, jnp.exp(jnp.maximum(diff, 0.0) * ld), 0.0)
            wts[h, pl.ds(pl.multiple_of(r * 64, 64), 64), :] = w
        return carry

    def piece(g, px, pz, rows, half=None):
        i0, n, _ = GROUPS[g]
        cc = pl.ds(0, 2) if half is None else pl.ds(half, 1)
        return buf.at[pl.ds(i0, n), px, pz, cc, pl.ds(*rows), :]

    def send(g, kind, ref, slot, where):
        rcopy(ref, ref, send_sem.at[g, kind], recv.at[g, slot], to[where]).start()

    def arrived(g, ref, slot):
        rcopy(ref, ref, send_sem.at[g, 0], recv.at[g, slot], sib).wait_recv()

    def relay(g, column, ref):
        rcopy(ref, ref, relay_send.at[g, column], relay_recv.at[g, column], sib).start()

    def own_arrived(g):
        i0, n, _ = GROUPS[g]
        ref = buf.at[pl.ds(i0, n), x, z, 1 - c]
        rcopy(ref, ref, own_send.at[g], own_recv.at[g], sib).wait_recv()

    def event_a(g, slot):
        pc = functools.partial(piece, g, rows=(0, GROUPS[g][2]))
        chain = lambda k, hop, way: 4 + (k * 4 + hop) * 2 + way
        columns = (x, xm, xp, x2)
        if slot < 3:
            k = slot + 1
            if slot >= 0:
                arrived(g, pc(columns[k], z), slot)
            for half in ((0, 1) if (g, slot) == (0, -1) else (None,)):
                ref = pc(columns[k], z, half=half)
                if slot < 0:
                    if half != 0:
                        own_arrived(g)
                    for o, where in enumerate(("xp", "xm", "x2")):
                        send(g, 0, ref, o, where)
                send(g, 1, ref, chain(k, 0, 0), "zp")
                send(g, 1, ref, chain(k, 0, 1), "zm")
            if slot >= 0:
                relay(g, k, ref)
            return
        k, hop, way = (slot - 4) // 8, (slot - 4) // 2 % 4, slot % 2
        pz = (z + (8 - hop - 1 if way == 0 else hop + 1)) % NZ
        ref = pc(columns[k], pz, half=way if hop == 3 else None)
        arrived(g, ref, slot)
        if hop < 3:
            part = pc(columns[k], pz, half=way if hop == 2 else None)
            send(g, 1, part, chain(k, hop + 1, way), ("zp", "zm")[way])
        relay(g, k, ref)

    def event_b(g, slot, last):
        _, _, a = GROUPS[g]
        pc = functools.partial(piece, g, rows=(a, SH - a))
        zs = (0, -1, 1, -2, 2, -3, 3, 4)

        def across(k):
            ref = pc(x, (z + 8 + zs[k]) % NZ)
            send(g, 1, ref, 8 + 4 * k, "xp")
            send(g, 1, ref, 9 + 4 * k, "xm")

        if slot < 0:
            for half in ((1, 0) if g == 0 else (None,)):
                if half != 1:
                    own_arrived(g)
                ref = pc(x, z, half=half)
                send(g, 0, ref, 0, "zp")
                send(g, 0, ref, 1, "zm")
                send(g, 1, ref, 8, "xp")
                send(g, 1, ref, 9, "xm")
        elif slot < 6:
            ref = pc(x, (z + 8 + zs[slot + 1]) % NZ)
            arrived(g, ref, slot)
            if slot < 4:
                send(g, 0, ref, slot + 2, ("zp", "zm")[slot % 2])
            if slot in (2, 3):
                half = pc(x, (z + 8 + zs[slot + 1]) % NZ, half=slot - 2)
                send(g, 0, half, slot + 4, ("zp2", "zm2")[slot - 2])
            across(slot + 1)
            relay(g, 0, ref)
        elif slot < 8:
            ref = pc(x, z4, half=slot - 6)
            arrived(g, ref, slot)
            relay(g, 0, ref)
            if last:
                across(7)
        else:
            k, j = (slot - 8) // 4, slot % 4
            pz = (z + 8 + zs[k]) % NZ
            ref = pc((xm, xp, x2, x2)[j], pz, half=None if j < 2 else j - 2)
            arrived(g, ref, slot)
            if j < 2:
                send(g, 1, pc((xm, xp)[j], pz, half=j), slot + 2, ("xp", "xm")[j])
            relay(g, (1, 2, 3, 3)[j], ref)

    def events(core, todo, seen):
        for g, slot in todo:
            if core == 0:
                event_a(g, slot)
            else:
                event_b(g, slot, (g, 13 - slot) in seen)
            seen.add((g, slot))

    def sizes(g, core):
        i0, n, a = GROUPS[g]
        if core == 0:
            return [buf.at[pl.ds(i0, n), pl.ds(0, 3), 0, :, pl.ds(0, a), :],
                    buf.at[pl.ds(i0, n), :, pl.ds(0, 7), :, pl.ds(0, a), :]]
        return [buf.at[pl.ds(i0, n), 0, pl.ds(0, 7), :, pl.ds(a, SH - a), :],
                buf.at[pl.ds(i0, n), pl.ds(0, 3), :, :, pl.ds(a, SH - a), :]]

    def column_size(g, core, column):
        i0, n, a = GROUPS[g]
        rows = pl.ds(0, a) if core == 0 else pl.ds(a, SH - a)
        return buf.at[pl.ds(i0, n), 0, pl.ds(0, 7 if column == 0 else 8), :, rows, :]

    def relays_arrived(g, column):
        for core in range(2):
            @pl.when(c == 1 - core)
            def _(core=core):
                ref = column_size(g, core, column)
                rcopy(ref, ref, relay_send.at[g, 0], relay_recv.at[g, column], sib).wait_recv()

    def sends_done(g):
        own_copy(g).wait_send()
        for core in range(2):
            @pl.when(c == core)
            def _(core=core):
                for kind, ref in enumerate(sizes(g, core)):
                    rcopy(ref, ref, send_sem.at[g, kind], recv.at[g, 0], sib).wait_send()
                for column in range(NX):
                    ref = column_size(g, core, column)
                    rcopy(ref, ref, relay_send.at[g, column], relay_recv.at[g, 0], sib).wait_send()

    def project(item, k):
        px = (x, xm, xp, x2)[k]
        cols = pl.ds(pl.multiple_of(px * KX, KX), KX)
        part = jnp.dot(xv[:, cols], buf[item, px].reshape(KX, F), preferred_element_type=F32)
        if k == 0:
            acc[item] = part
        else:
            acc[item] += part

    def silu(v):
        return v * jax.nn.sigmoid(v)

    def local_state():
        for h in range(2):
            tail = jnp.exp((T - 1.0 - pos((T, HD), 0)) * log_decay[h])
            cols = pl.ds(HD * h, HD)
            kt = (kv[0, :, cols].astype(F32) * tail).astype(BF)
            state[h] = lax.dot_general(kt, kv[1, :, cols], (((0,), (0,)), ((), ())), preferred_element_type=F32)

    whole = lambda n: jnp.exp((n * T) * jnp.where(c == 0, log_decay[0], log_decay[1]))

    def scan_open():
        rcopy(state.at[1 - c], sx, st_send.at[0, 0], st_recv.at[0, 0], sib).start()

    def scan_chip():
        rcopy(state.at[1 - c], sx, st_send.at[0, 0], st_recv.at[0, 0], sib).wait_recv()
        mine, other = state[c], sx[...]
        first = jnp.where(c == 0, mine, other)
        stg[0] = first
        stg[1] = whole(1.0) * first + jnp.where(c == 0, other, mine)
        stg[2] = jnp.zeros_like(first)

    steps = (((z_pair,), z % 2, 1, 0), (z_four, z // 2, 2, z % 2), (x_four, x, 8, z))

    def scan_send(k):
        snd[k] = stg[1].astype(BF)
        for o, other in enumerate(steps[k][0]):
            rcopy(snd.at[k], rcv.at[k, o], st_send.at[1 + k, o], st_recv.at[1 + k, o], other).start()

    def scan_step(k):
        others, place, span, reach = steps[k]
        count = len(others) + 1
        chips = lambda n: whole(2.0 * jnp.asarray(n, jnp.int32).astype(F32))
        tot = stg[1] * chips((count - 1 - place) * span)
        before = stg[2]
        for o, other in enumerate(others):
            rcopy(snd.at[k], rcv.at[k, o], st_send.at[1 + k, o], st_recv.at[1 + k, o], other).wait_recv()
            got = rcv[k, o].astype(F32)
            source = (place + count - 1 - o) % count
            before += jnp.where(place > o, chips(o * span + reach), 0.0) * got
            tot += chips((count - 1 - source) * span) * got
        stg[1] = tot
        stg[2] = before

    def scan_end():
        low = stg[2]
        high = whole(1.0) * low + stg[0]
        pri[c] = jnp.where(c == 0, low, high)
        stg[3] = jnp.where(c == 0, high, low)
        rcopy(stg.at[3], pri.at[c], st_send.at[0, 1], st_recv.at[0, 1], sib).start()

    def scan_close():
        rcopy(stg.at[3], pri.at[1 - c], st_send.at[0, 1], st_recv.at[0, 1], sib).wait_recv()

    def intra(h, r):
        cols = pl.ds(HD * h, HD)
        rows = pl.ds(128 * r, 128)
        seen = 128 * (r + 1)
        scores = lax.dot_general(qv[rows, cols], kv[0, :seen, cols], (((1,), (1,)), ((), ())), preferred_element_type=F32)
        probs = (scores * wts[h, rows, :seen]).astype(BF)
        att[rows, cols] = jnp.dot(probs, kv[1, :seen, cols], preferred_element_type=F32)

    def inter(h):
        cols = pl.ds(HD * h, HD)
        into = jnp.exp((pos((T, HD), 0) + 1.0) * log_decay[h])
        prior = pri[h]
        top = prior.astype(BF)
        rest = (prior - top.astype(F32)).astype(BF)
        query = qv[:, cols]
        got = jnp.dot(query, top, preferred_element_type=F32) + jnp.dot(query, rest, preferred_element_type=F32)
        full = att[:, cols] + into * got
        scale = lax.rsqrt(jnp.mean(full * full, axis=1, keepdims=True) + 1e-06)
        att[:, cols] = full * scale * gain_ref[:, HD * h:HD * (h + 1)]

    def hcopy(src_y, r, lo, n, slot):
        ref = hid.at[src_y, pl.ds(128 * r + lo, n), :]
        return rcopy(ref, ref, h_send.at[r, slot], h_recv.at[r, slot], to_y[slot % 2])

    def gate(r):
        rows = pl.ds(128 * r, 128)
        hid[y, rows, :] = (att[rows, :] * jax.nn.sigmoid(acc[3, rows, :])).astype(BF)
        hcopy(y, r, 0, 128, 0).start()
        hcopy(y, r, 0, 128, 1).start()

    def forward(r):
        hcopy(ym, r, 0, 128, 0).wait_recv()
        hcopy(ym, r, 0, 64, 2).start()
        hcopy(yp, r, 0, 128, 1).wait_recv()
        hcopy(yp, r, 64, 64, 3).start()

    def far(r):
        hcopy(y2, r, 0, 64, 2).wait_recv()
        hcopy(y2, r, 64, 64, 3).wait_recv()

    def out_part(py, first):
        for j in range(6):
            cols = pl.ds(F * j, F)
            w = buf[4, py, :, :, 16 * j:16 * (j + 1), :].reshape(F, F)
            part = jnp.dot(hid[py], w, preferred_element_type=F32)
            if first:
                oacc[:, cols] = part
            else:
                oacc[:, cols] += part

    def out_last(lo, n):
        rows = pl.ds(lo, n)
        for j in range(6):
            cols = pl.ds(F * j, F)
            w = buf[4, y2, :, :, 16 * j:16 * (j + 1), :].reshape(F, F)
            part = jnp.dot(hid[y2, rows, :], w, preferred_element_type=F32)
            out_ref[rows, cols] = (oacc[rows, cols] + part).astype(BF)

    def finish_k():
        kv[0] = silu(acc[0]).astype(BF)

    def finish_v():
        kv[1] = silu(acc[1]).astype(BF)

    def finish_q():
        qv[...] = silu(acc[2]).astype(BF)

    def weights(g, k):
        relays_arrived(g, k)
        if (g, k) == (0, 0):
            x_load.wait()

    def act(name):
        kind, n = name.rstrip("0123"), name[-1]
        n = int(n) if n.isdigit() else None
        if kind == "table":
            for g in range(1, len(GROUPS)):
                share(g)
            read_decays()
            lax.fori_loop(0, T // 64, table, 0)
        elif kind in "KVQG":
            item = "KVQG".index(kind)
            if kind != "V":
                weights((0, 0, 1, 2)[item], n)
            project(item, n)
        elif kind == "fin" + name[-1]:
            (finish_k if n is None and name[-1] == "K" else finish_v if name[-1] == "V" else finish_q)()
        elif kind == "state":
            local_state()
            scan_open()
        elif kind == "chip":
            scan_chip()
            scan_send(0)
        elif kind == "st":
            scan_step(n)
            if n < 2:
                scan_send(n + 1)
            else:
                scan_end()
        elif kind == "intra":
            for r in range(4):
                intra(n, r)
        elif kind == "inter":
            scan_close()
            for h in range(2):
                inter(h)
        elif kind == "gate":
            gate(n)
        elif kind == "fwd":
            forward(n)
        elif kind == "out":
            if n == 0:
                for k in range(NX):
                    weights(3, k)
            if n < 3:
                out_part((y, ym, yp)[n], n == 0)
            else:
                for half in range(2):
                    far(2 * half)
                    far(2 * half + 1)
                    out_last(256 * half, 256)

    seen = (set(), set())
    for name, *todo in PLAN:
        for core in range(2):
            if todo[core]:
                @pl.when(c == core)
                def _(core=core, todo=todo):
                    events(core, todo[core], seen[core])
        if name:
            act(name)

    for g in range(len(GROUPS)):
        sends_done(g)
    rcopy(state.at[1 - c], sx, st_send.at[0, 0], st_recv.at[0, 0], sib).wait_send()
    rcopy(stg.at[3], pri.at[c], st_send.at[0, 1], st_recv.at[0, 1], sib).wait_send()
    for k in range(3):
        for o, other in enumerate(steps[k][0]):
            rcopy(snd.at[k], rcv.at[k, o], st_send.at[1 + k, o], st_recv.at[1 + k, o], other).wait_send()
    for r in range(4):
        hcopy(y, r, 0, 128, 0).wait_send()
        hcopy(y, r, 0, 128, 1).wait_send()
        hcopy(ym, r, 0, 64, 2).wait_send()
        hcopy(yp, r, 64, 64, 3).wait_send()

def shards(inputs, proj_weight, decay_codes, norm_gain, out_weight):
    vmem = pltpu.VMEM
    dma = pltpu.SemaphoreType.DMA
    hbm = pl.BlockSpec(memory_space=pltpu.HBM)
    ng = len(GROUPS)
    args = (inputs, proj_weight, decay_codes, norm_gain.reshape(1, F), out_weight)
    args = [pltpu.with_memory_space_constraint(a, pltpu.HBM) for a in args]
    return pl.pallas_call(
        kernel,
        out_shape=jax.ShapeDtypeStruct((T, 1536), BF),
        in_specs=[hbm] * 5,
        out_specs=pl.BlockSpec(memory_space=vmem),
        scratch_shapes=[
            pltpu.SMEM((2,), jnp.int32),
            vmem((1, F), F32),
            vmem((5, NX, NZ, 2, SH, F), BF),
            vmem((T, D), BF),
            vmem((2, T, T), F32),
            vmem((4, T, F), F32),
            vmem((2, T, F), BF),
            vmem((T, F), BF),
            vmem((T, F), F32),
            vmem((NY, T, F), BF),
            vmem((T, 1536), F32),
            vmem((2, HD, HD), F32),
            vmem((HD, HD), F32),
            vmem((3, HD, HD), BF),
            vmem((3, 3, HD, HD), BF),
            vmem((4, HD, HD), F32),
            vmem((2, HD, HD), F32),
            dma((12,)),
            dma((ng,)),
            dma((ng,)),
            dma((ng, NSLOT)),
            dma((ng, NX)),
            dma((ng, NX)),
            dma((ng, 2)),
            dma((4, 3)),
            dma((4, 3)),
            dma((4, 4)),
            dma((4, 4)),
        ],
        compiler_params=pltpu.CompilerParams(collective_id=0, has_side_effects=True, vmem_limit_bytes=52 * 2 ** 20),
        name="lightning",
    )(*args)


def solution(mesh):
    in_specs = (P("seq", None), P(None, "seq", "tp"), P("tp"), P("tp"), P("seq", "tp"))
    out_specs = P("seq", "tp")
    return jax.shard_map(shards, mesh=mesh, in_specs=in_specs, out_specs=out_specs, check_vma=False)
```
